32 devices in a mesh: batch: 8 (over z, y), ctx: 4 (over x, core).
Axes of the slice: x: 2, y: 2, z: 4, core: 2. Of those that a mesh axis runs over, the one named last changes fastest.
Arguments:
- block_input: bfloat16 [8, 1024, 2048], P('batch', 'ctx'), may hold values from -6 to 6
- output_grad: bfloat16 [8, 1024, 2048], P('batch', 'ctx'), may hold values from -6 to 6
- documents: int32 [8, 1024], P('batch'), may hold values from 0 to 3, as said below
- span_order: int32 [8, 4], P('batch'), may hold values from 0 to 3, as said below
- attention_norm_gain: bfloat16 [2048], P(('batch', 'ctx')), may hold values from 0.5 to 1.5
- attention_norm_bias: bfloat16 [2048], P(('batch', 'ctx')), may hold values from -1.75 to 1.75
- query_key_value_weight: bfloat16 [2048, 6144], P(('batch', 'ctx')), may hold values from -0.125 to 0.125
- query_key_value_bias: bfloat16 [6144], P(('batch', 'ctx')), may hold values from -1.75 to 1.75
- dense_weight: bfloat16 [2048, 2048], P(('batch', 'ctx')), may hold values from -2 to 2
- dense_bias: bfloat16 [2048], P(('batch', 'ctx')), may hold values from -1.75 to 1.75
- mlp_norm_gain: bfloat16 [2048], P(('batch', 'ctx')), may hold values from 0.5 to 1.5
- mlp_norm_bias: bfloat16 [2048], P(('batch', 'ctx')), may hold values from -1.75 to 1.75
- to_hidden_weight: bfloat16 [2048, 8192], P(('batch', 'ctx')), may hold values from -0.125 to 0.125
- to_hidden_bias: bfloat16 [8192], P(('batch', 'ctx')), may hold values from -3 to 3
- from_hidden_weight: bfloat16 [8192, 2048], P(('batch', 'ctx')), may hold values from -0.0625 to 0.0625
- from_hidden_bias: bfloat16 [2048], P(('batch', 'ctx')), may hold values from -1.75 to 1.75
Outputs:
- block_output: bfloat16 [8, 1024, 2048], P('batch', 'ctx')
- input_grad: bfloat16 [8, 1024, 2048], P('batch', 'ctx')
- attention_norm_gain_grad: float32 [2048], P(('batch', 'ctx'))
- attention_norm_bias_grad: float32 [2048], P(('batch', 'ctx'))
- query_key_value_weight_grad: float32 [2048, 6144], P(('batch', 'ctx'))
- query_key_value_bias_grad: float32 [6144], P(('batch', 'ctx'))
- dense_weight_grad: float32 [2048, 2048], P(('batch', 'ctx'))
- dense_bias_grad: float32 [2048], P(('batch', 'ctx'))
- mlp_norm_gain_grad: float32 [2048], P(('batch', 'ctx'))
- mlp_norm_bias_grad: float32 [2048], P(('batch', 'ctx'))
- to_hidden_weight_grad: float32 [2048, 8192], P(('batch', 'ctx'))
- to_hidden_bias_grad: float32 [8192], P(('batch', 'ctx'))
- from_hidden_weight_grad: float32 [8192, 2048], P(('batch', 'ctx'))
- from_hidden_bias_grad: float32 [2048], P(('batch', 'ctx'))
The draws below stay inside these ranges and needn't reach their ends.
Inputs may be any that keep to these rules, and one draw needn't show every extreme that they name: `span_order`: each row is a permutation of 0 to 3. documents[s, c * 256 + i] is the document of the token at position span_order[s, c] * 256 + i of sequence s; documents are numbered from 0 upward in order of position.
All inputs are finite; a program needn't handle non-finite values.
Results may differ from the reference program's by a relative error of at most 0.0096.
Values may be sent and summed in bfloat16 or wider, within the bound.
No kernel may reach another device: no remote copies, remote signals or barrier semaphores. Data moves between devices by JAX's collectives and lax.ppermute only.
A program may use at most 448 MiB of HBM per device.

```python
import jax
import jax.numpy as jnp
from jax import lax

D = 2048
H = 16
HD = 128
FF = 8192
ROT = 32
SPAN = 256
SEQS = 8
LENGTH = 1024


def order_table(key):
    pieces = LENGTH // SPAN
    seq_keys = jax.random.split(key, SEQS)
    return jax.vmap(lambda single: jax.random.permutation(single, pieces))(seq_keys).astype(jnp.int32)


def draw_span_order(key, part):
    table = order_table(key)
    return table


def draw_documents(key, part):
    table = order_table(key)
    key = jax.random.fold_in(key, 11)
    key_one, key_two, key_three = jax.random.split(key, 3)
    half_span = SPAN // 2
    first_cut = jax.random.randint(key_one, (SEQS, 1), 1, half_span)
    second_cut = jax.random.randint(key_two, (SEQS, 1), half_span, SPAN)
    third_cut = jax.random.randint(key_three, (SEQS, 1), LENGTH - SPAN + 1, LENGTH)
    places = jnp.arange(LENGTH, dtype=jnp.int32)[None, :]
    ordered = (places >= first_cut).astype(jnp.int32) + (places >= second_cut).astype(jnp.int32) + (places >= third_cut).astype(jnp.int32)
    offsets = jnp.arange(SPAN, dtype=jnp.int32)
    stored = (table[:, :, None] * SPAN + offsets[None, None, :]).reshape(SEQS, LENGTH)
    return jnp.take_along_axis(ordered, stored, axis=1).astype(jnp.int32)


def block_levels(own_key, shape, cuts, least, high):
    def one(position, shards_of):
        steps = jax.random.uniform(jax.random.fold_in(jax.random.fold_in(own_key, 6), position), (shards_of,), jnp.float32, least / len(cuts), high / len(cuts))
        return jnp.repeat(jnp.exp(steps), shape[position] // shards_of).reshape((-1,) + (1,) * (len(shape) - position - 1))

    gain = one(*cuts[0])
    for cut in cuts[1:]:
        gain = gain * one(*cut)
    return gain


def bell_draw(own_key, extent, width, limit, cuts=(), kind=jnp.bfloat16):
    array = jax.random.normal(own_key, extent, jnp.float32) * width
    if len(cuts) > 0:
        array = block_levels(own_key, extent, cuts, -0.22, 0.18) * array
    return jnp.clip(array, min=-limit, max=limit).astype(kind)


def setup_inputs(seed: int = 0) -> dict:
    arg_keys = jax.random.split(jax.random.key(seed), 17)
    block_input = bell_draw(arg_keys[0], (SEQS, LENGTH, D), 1.0, 6.0, ((0, 8), (1, 4)))
    output_grad = bell_draw(arg_keys[1], (SEQS, LENGTH, D), 1.0, 6.0, ((0, 8), (1, 4)))
    documents = draw_documents(jax.random.fold_in(arg_keys[16], 71), 0)
    span_order = draw_span_order(jax.random.fold_in(arg_keys[16], 71), 0)
    attention_norm_gain = jnp.clip(1.0 + 0.1 * jax.random.normal(arg_keys[4], (D,), jnp.float32), 0.5, 1.5).astype(jnp.bfloat16)
    attention_norm_bias = bell_draw(arg_keys[5], (D,), 0.3, 1.75, ((0, 32),))
    query_key_value_weight = bell_draw(arg_keys[6], (D, 3 * D), D ** -0.5, 0.125, ((0, 32),))
    query_key_value_bias = bell_draw(arg_keys[7], (3 * D,), 0.3, 1.75, ((0, 32),))
    dense_weight = bell_draw(arg_keys[8], (D, D), (max(D // 256, 1)) ** -0.5, 2.0, ((0, 32),))
    dense_bias = bell_draw(arg_keys[9], (D,), 0.3, 1.75, ((0, 32),))
    mlp_norm_gain = jnp.clip(1.0 + 0.1 * jax.random.normal(arg_keys[10], (D,), jnp.float32), 0.5, 1.5).astype(jnp.bfloat16)
    mlp_norm_bias = bell_draw(arg_keys[11], (D,), 0.3, 1.75, ((0, 32),))
    to_hidden_weight = bell_draw(arg_keys[12], (D, FF), D ** -0.5, 0.125, ((0, 32),))
    to_hidden_bias = bell_draw(arg_keys[13], (FF,), 0.5, 3.0, ((0, 32),))
    from_hidden_weight = bell_draw(arg_keys[14], (FF, D), FF ** -0.5, 0.0625, ((0, 32),))
    from_hidden_bias = bell_draw(arg_keys[15], (D,), 0.3, 1.75, ((0, 32),))
    return dict(block_input=block_input, output_grad=output_grad, documents=documents, span_order=span_order, attention_norm_gain=attention_norm_gain, attention_norm_bias=attention_norm_bias, query_key_value_weight=query_key_value_weight, query_key_value_bias=query_key_value_bias, dense_weight=dense_weight, dense_bias=dense_bias, mlp_norm_gain=mlp_norm_gain, mlp_norm_bias=mlp_norm_bias, to_hidden_weight=to_hidden_weight, to_hidden_bias=to_hidden_bias, from_hidden_weight=from_hidden_weight, from_hidden_bias=from_hidden_bias)


epsilon = 1e-05
neg_large = -1e+30
theta_base = 10000.0
highest = lax.Precision.HIGHEST

@jax.custom_vjp
def low(v):
    return lax.optimization_barrier(v.astype(jnp.bfloat16)).astype(jnp.float32)

@jax.custom_vjp
def low_back(v):
    return v

def low_keep(v):
    return (low(v), None)

def low_pass(kept, grad):
    return (grad,)

def back_keep(v):
    return (v, None)

def back_low(kept, grad):
    return (low(grad),)
low.defvjp(low_keep, low_pass)
low_back.defvjp(back_keep, back_low)

def matmul(left_side, right_side):
    return jnp.dot(left_side, right_side, precision=highest, preferred_element_type=jnp.float32)

def layer_norm(values, scaling, offset_row):
    centre = values - lax.optimization_barrier(jnp.mean(values, axis=-1, keepdims=True))
    spread = lax.optimization_barrier(jnp.mean(centre * centre, axis=-1, keepdims=True))
    return centre * lax.rsqrt(spread + epsilon) * scaling + offset_row

def rotate(values, positions, direction):
    half_rot = ROT // 2
    powers = jnp.arange(half_rot, dtype=jnp.float32) * (2.0 / ROT)
    inverse = jnp.power(theta_base, -powers)
    angles = positions.astype(jnp.float32)[:, None] * inverse[None, :]
    cosine = jnp.cos(angles)[:, None, :]
    sine_part = direction * jnp.sin(angles)[:, None, :]
    first_half = values[..., :half_rot]
    second = values[..., half_rot:ROT]
    remainder = values[..., ROT:]
    return jnp.concatenate([first_half * cosine - second * sine_part, second * cosine + first_half * sine_part, remainder], axis=-1)

def one_sequence(params, tokens_in, positions, documents):
    norm_gain, norm_shift, joined_weight, joined_shift, dense_w, dense_shift, norm_gain_two, norm_shift_two, hidden_w, hidden_shift, back_w, back_shift = params
    length = tokens_in.shape[0]
    normed = low(layer_norm(tokens_in, norm_gain, norm_shift))
    joined_lin = low_back(matmul(normed, joined_weight) + joined_shift)
    query_part = low(rotate(joined_lin[:, :D].reshape(length, H, HD), positions, 1.0))
    key_part = low(rotate(joined_lin[:, D:2 * D].reshape(length, H, HD), positions, 1.0))
    value_part = low(joined_lin[:, 2 * D:].reshape(length, H, HD))
    scores = low_back(jnp.einsum('qhd,khd->hqk', query_part, key_part, precision=highest) * HD ** (-0.5))
    allowed = (positions[None, :] <= positions[:, None]) & (documents[None, :] == documents[:, None])
    scores = jnp.where(allowed[None], scores, neg_large)
    highest_score = lax.optimization_barrier(jnp.max(scores, axis=-1, keepdims=True))
    weights = jnp.exp(scores - highest_score)
    weights = weights / lax.optimization_barrier(jnp.sum(weights, axis=-1, keepdims=True))
    mixed = jnp.einsum('hqk,khd->qhd', low(weights), value_part, precision=highest).reshape(length, D)
    mixed = low(low_back(mixed))
    attention = matmul(mixed, dense_w) + dense_shift
    normed_two = low(layer_norm(tokens_in, norm_gain_two, norm_shift_two))
    hidden = low_back(matmul(normed_two, hidden_w) + hidden_shift)
    activated = low(jax.nn.gelu(hidden, approximate=False))
    feed_out = matmul(activated, back_w) + back_shift
    return tokens_in + attention + feed_out

def reference(block_input, output_grad, documents, span_order, attention_norm_gain, attention_norm_bias, query_key_value_weight, query_key_value_bias, dense_weight, dense_bias, mlp_norm_gain, mlp_norm_bias, to_hidden_weight, to_hidden_bias, from_hidden_weight, from_hidden_bias):
    params = tuple((tensor.astype(jnp.float32) for tensor in (attention_norm_gain, attention_norm_bias, query_key_value_weight, query_key_value_bias, dense_weight, dense_bias, mlp_norm_gain, mlp_norm_bias, to_hidden_weight, to_hidden_bias, from_hidden_weight, from_hidden_bias)))
    offsets = jnp.arange(SPAN, dtype=jnp.int32)
    positions = (span_order[:, :, None] * SPAN + offsets[None, None, :]).reshape(SEQS, LENGTH).astype(jnp.int32)
    checked = jax.checkpoint(one_sequence)

    def forward(weight_set, tokens_all):
        return lax.map(lambda entries: checked(weight_set, entries[0], entries[1], entries[2]), (tokens_all, positions, documents))
    outputs, pullback = jax.vjp(forward, params, block_input.astype(jnp.float32))
    weight_grads, input_grad = pullback(output_grad.astype(jnp.float32))
    return (outputs.astype(jnp.bfloat16), input_grad.astype(jnp.bfloat16), weight_grads[0], weight_grads[1], weight_grads[2], weight_grads[3], weight_grads[4], weight_grads[5], weight_grads[6], weight_grads[7], weight_grads[8], weight_grads[9], weight_grads[10], weight_grads[11])
```

```python
import functools

import jax
import jax.numpy as jnp
from jax import lax
from jax.experimental import pallas as pl
from jax.experimental.pallas import tpu as pltpu
from jax.sharding import Mesh, PartitionSpec as P

D = 2048
H = 16
HD = 128
ROT = 32
FF = 8192
EPS = 1e-05
NEG = -1e30
THETA = 10000.0
BF = jnp.bfloat16
F32 = jnp.float32
AXES = ("zh", "zl", "y", "x", "core")
QB = 256


def flip(v, axis):
    return lax.ppermute(v, axis, [(0, 1), (1, 0)])


def dot(a, b, ca, cb):
    return lax.dot_general(a, b, (((ca,), (cb,)), ((), ())), preferred_element_type=F32)


def turn(v, cos, sin):
    lane = lax.broadcasted_iota(jnp.int32, v.shape, 1)
    half = ROT // 2
    swapped = jnp.where(lane < half, pltpu.roll(v, HD - half, 1), pltpu.roll(v, half, 1))
    return v * cos + swapped * sin


def attention_kernel(
    q, k, v, do, cq, sq, ck, sk, pq, eq, pk, ek, o, dq, dk, dv, ks, vs, dka, dva
):
    i = pl.program_id(2)
    scale = HD ** (-0.5)

    @pl.when(i == 0)
    def _():
        ks[...] = turn(k[...], ck[...], sk[...]).astype(BF)
        vs[...] = v[...].astype(BF)
        dka[...] = jnp.zeros_like(dka)
        dva[...] = jnp.zeros_like(dva)

    qr = turn(q[...], cq[...], sq[...]).astype(BF)
    s = dot(qr, ks[...], 1, 1) * scale
    allowed = (pk[...] <= pq[...]) & (ek[...] == eq[...])
    s = jnp.where(allowed, s, NEG)
    e = jnp.exp(s - jnp.max(s, axis=-1, keepdims=True))
    p = e / jnp.sum(e, axis=-1, keepdims=True)
    low = p.astype(BF)
    o[...] = dot(low, vs[...], 1, 0).astype(BF)
    dp = dot(do[...], vs[...], 1, 1)
    ds = (p * (dp - jnp.sum(p * dp, axis=-1, keepdims=True))).astype(BF)
    dq[...] = turn(dot(ds, ks[...], 1, 0) * scale, cq[...], -sq[...]).astype(BF)
    dva[...] += dot(low, do[...], 0, 0)
    dka[...] += dot(ds, qr, 0, 0)

    @pl.when(i == pl.num_programs(2) - 1)
    def _():
        dk[...] = turn(dka[...] * scale, ck[...], -sk[...]).astype(BF)
        dv[...] = dva[...].astype(BF)


def attention(joined, grad, cos, sin, pos, doc):
    seqs, length, _ = joined.shape
    heads = grad.shape[2] // HD
    part = lambda off: pl.BlockSpec((None, QB, HD), lambda s, h, i: (s, i, off + h))
    whole = lambda off: pl.BlockSpec((None, length, HD), lambda s, h, i: (s, 0, off + h))
    tq = pl.BlockSpec((None, QB, HD), lambda s, h, i: (s, i, 0))
    tk = pl.BlockSpec((None, length, HD), lambda s, h, i: (s, 0, 0))
    col = pl.BlockSpec((None, QB, 1), lambda s, h, i: (s, i, 0))
    row = pl.BlockSpec((None, 1, length), lambda s, h, i: (s, 0, 0))
    out = jax.ShapeDtypeStruct((seqs, length, heads * HD), BF)
    return pl.pallas_call(
        attention_kernel,
        grid=(seqs, heads, length // QB),
        in_specs=[part(0), whole(heads), whole(2 * heads), part(0), tq, tq, tk, tk, col, col, row, row],
        out_specs=[part(0), part(0), whole(0), whole(0)],
        out_shape=[out] * 4,
        scratch_shapes=[
            pltpu.VMEM((length, HD), BF),
            pltpu.VMEM((length, HD), BF),
            pltpu.VMEM((length, HD), F32),
            pltpu.VMEM((length, HD), F32),
        ],
        compiler_params=pltpu.CompilerParams(vmem_limit_bytes=40 * 2**20),
        cost_estimate=pl.CostEstimate(
            flops=seqs * heads * length * length * HD * 14,
            bytes_accessed=seqs * length * heads * HD * 24,
            transcendentals=seqs * heads * length * length,
        ),
    )(
        joined, joined, joined, grad, cos, sin, cos, sin,
        pos[:, :, None], doc[:, :, None], pos[:, None, :], doc[:, None, :],
    )


def gather_tokens(v):
    far = flip(v, "zl")
    near_x = flip(v, "x")
    far_x = flip(far, "x")
    blocks = []
    for b in (v, near_x, far, far_x):
        blocks += [b, flip(b, "core")]
    return jnp.concatenate(blocks, axis=0)


def reduce_tokens(p, span):
    p = p.reshape(2, 2, 2, span, -1)

    def near(half):
        return [half[b, 0].astype(F32) + flip(half[b, 1], "core").astype(F32) for b in (1, 0)]

    away, mine = near(p[1])
    total = mine + flip(away.astype(BF), "x").astype(F32)
    from_far = flip(total.astype(BF), "zl")
    away, mine = near(p[0])
    total = mine + flip(away.astype(BF), "x").astype(F32)
    return total + from_far.astype(F32)


def gather_replicas(v, copies):
    p, r, c = v.shape
    if copies != 2:
        w = lax.all_gather(v, ("zh", "y"), axis=0, tiled=False)
        return w.reshape(2, copies, p, r, c).transpose(0, 2, 1, 3, 4)
    zh, y = lax.axis_index("zh"), lax.axis_index("y")
    far = flip(v, "zh")
    pieces = {(0, 0): v, (0, 1): flip(v, "y"), (1, 0): far, (1, 1): flip(far, "y")}
    w = jnp.zeros((2, p, 2, r, c), v.dtype)
    for (a, b), piece in pieces.items():
        w = lax.dynamic_update_slice(w, piece[None, :, None], (zh ^ a, 0, y ^ b, 0, 0))
    return w


def reduce_replicas(v, copies):
    h, p, _, r, c = v.shape
    if copies != 2:
        w = v.transpose(0, 2, 1, 3, 4).reshape(h * copies, p, r, c)
        return lax.psum_scatter(w, ("zh", "y"), scatter_dimension=0, tiled=False)
    zh, y = lax.axis_index("zh"), lax.axis_index("y")
    part = lambda a, b: lax.dynamic_slice(v, (zh ^ a, 0, y ^ b, 0, 0), (1, p, 1, r, c)).reshape(p, r, c)
    far = part(1, 0) + flip(part(1, 1).astype(BF), "y").astype(F32)
    from_far = flip(far.astype(BF), "zh")
    near = part(0, 0) + flip(part(0, 1).astype(BF), "y").astype(F32)
    return near + from_far.astype(F32)


def gather_small(v, copies):
    if copies != 2:
        return lax.all_gather(v, AXES, axis=0, tiled=False)
    v = v[None]
    for axis in reversed(AXES):
        other, first = flip(v, axis), lax.axis_index(axis) == 0
        v = jnp.concatenate([jnp.where(first, v, other), jnp.where(first, other, v)], axis=0)
    return v


def reduce_small(v, copies):
    if copies != 2:
        return lax.psum_scatter(v, AXES, scatter_dimension=0, tiled=False)
    for axis in AXES:
        n, first = v.shape[0] // 2, lax.axis_index(axis) == 0
        v = jnp.where(first, v[:n], v[n:]) + flip(jnp.where(first, v[n:], v[:n]), axis)
    return v[0]


def gather_dense(w, copies):
    core, x = lax.axis_index("core"), lax.axis_index("x")
    if copies != 2:
        w = lax.all_gather(w, ("zh", "y", "x", "core"), axis=0, tiled=True)
        w = w.reshape(2, 2, 2, HD, D)
        w = lax.dynamic_slice(w, (core, 0, x, 0, 0), (1, 2, 1, HD, D))
        return w.reshape(2 * HD, D)
    w = gather_replicas(w[None], copies)[:, 0]
    first = core == 0
    keep = jnp.where(first, w[0], w[1])
    other = flip(jnp.where(first, w[1], w[0]), "core")
    low, high = jnp.where(first, keep, other), jnp.where(first, other, keep)
    return jnp.stack([low, high], axis=1).reshape(2 * HD, D)


def reduce_dense(g, copies):
    core, x = lax.axis_index("core"), lax.axis_index("x")
    if copies != 2:
        w = jnp.zeros((2, 2, 2, HD, D), F32)
        w = lax.dynamic_update_slice(w, g.reshape(1, 2, 1, HD, D), (core, 0, x, 0, 0))
        w = w.reshape(-1, D)
        return lax.psum_scatter(w, ("zh", "y", "x", "core"), scatter_dimension=0, tiled=True)
    g = g.reshape(2, 2, HD // 2, D)
    first = core == 0
    keep = jnp.where(first, g[:, 0], g[:, 1])
    other = flip(jnp.where(first, g[:, 1], g[:, 0]).astype(BF), "core").astype(F32)
    w = jnp.stack([jnp.where(first, keep, other), jnp.where(first, other, keep)])
    return reduce_replicas(w[:, None], copies)[0]


def swap_shards(v):
    return lax.all_to_all(v, ("zl", "x", "core"), 0, 0, tiled=True)


def shards(
    copies,
    block_input,
    output_grad,
    documents,
    span_order,
    attention_norm_gain,
    attention_norm_bias,
    query_key_value_weight,
    query_key_value_bias,
    dense_weight,
    dense_bias,
    mlp_norm_gain,
    mlp_norm_bias,
    to_hidden_weight,
    to_hidden_bias,
    from_hidden_weight,
    from_hidden_bias,
):
    span = block_input.shape[1]
    count = 16 * copies
    rows = D // count
    units = FF // count
    length = 4 * span
    zl, x, core = (lax.axis_index(a) for a in ("zl", "x", "core"))
    own_in, own_grad = block_input[0], output_grad[0]

    wide = query_key_value_weight.reshape(rows, 3, 2, 2, 2, 2, HD)
    wide = wide.transpose(3, 5, 2, 0, 1, 4, 6).reshape(8, rows, 6 * HD)
    tall = to_hidden_weight.reshape(rows, 2, 2, copies, 2, 2, units)
    tall = tall.transpose(2, 4, 5, 0, 1, 3, 6).reshape(8, rows, FF // 8)
    both = swap_shards(jnp.concatenate([wide, tall], axis=2).reshape(8 * rows, -1))
    both = both.reshape(2, 4 * rows, -1)
    joined_w = gather_replicas(both[:, :, : 6 * HD], copies).reshape(D, 6 * HD)
    hidden_w = gather_replicas(both[:, :, 6 * HD :], copies).reshape(D, FF // 8)
    dense_w = gather_dense(dense_weight, copies)
    back_w = gather_replicas(from_hidden_weight[None], copies).reshape(FF // 8, D)

    small = gather_small(
        jnp.concatenate(
            [
                attention_norm_gain,
                attention_norm_bias,
                dense_bias,
                mlp_norm_gain,
                mlp_norm_bias,
                from_hidden_bias,
                query_key_value_bias,
                to_hidden_bias,
            ]
        ),
        copies,
    ).astype(F32)
    take = lambda a, n: small[:, a : a + n].reshape(-1)
    gain_one, shift_one, dense_shift, gain_two, shift_two, back_shift = (
        take(j * rows, rows) for j in range(6)
    )
    joined_shift = take(6 * rows, 3 * rows).reshape(3, 2, 2, 2, 2, HD)
    joined_shift = lax.dynamic_slice(joined_shift, (0, core, zl, 0, x, 0), (3, 1, 1, 2, 1, HD))
    joined_shift = joined_shift.reshape(6 * HD)
    hidden_shift = take(9 * rows, units).reshape(2, 2, copies, 2, 2, units)
    hidden_shift = lax.dynamic_slice(
        hidden_shift, (0, zl, 0, x, core, 0), (2, 1, copies, 1, 1, units)
    ).reshape(FF // 8)

    tokens = gather_tokens(own_in)
    upstream = gather_tokens(own_grad)
    facts = jnp.concatenate([documents[0], span_order[0]])
    offsets = jnp.arange(span, dtype=jnp.int32)
    pos, doc = [], []
    for known in (facts, flip(facts, "zl")):
        for b in (0, 1):
            for c in (0, 1):
                block = (x ^ b) * 2 + (core ^ c)
                doc.append(lax.dynamic_slice(known, (block * span,), (span,)))
                pos.append(lax.dynamic_slice(known, (length + block,), (1,)) * span + offsets)
    pos = jnp.concatenate(pos).reshape(2, length)
    doc = jnp.concatenate(doc).reshape(2, length)
    inverse = jnp.power(THETA, -jnp.arange(ROT // 2, dtype=F32) * (2.0 / ROT))
    angles = pos.astype(F32)[:, :, None] * inverse
    cosine, sine = jnp.cos(angles), jnp.sin(angles)
    rest = jnp.zeros((2, length, HD - ROT), F32)
    cos_table = jnp.concatenate([cosine, cosine, rest + 1.0], axis=-1)
    sin_table = jnp.concatenate([-sine, sine, rest], axis=-1)

    tokens_wide = tokens.astype(F32)
    centre = tokens_wide - jnp.mean(tokens_wide, axis=-1, keepdims=True)
    spread = lax.rsqrt(jnp.mean(centre * centre, axis=-1, keepdims=True) + EPS)
    normal = centre * spread
    normed_one = (normal * gain_one + shift_one).astype(BF)
    normed_two = (normal * gain_two + shift_two).astype(BF)

    joined = dot(normed_one, joined_w, 1, 0) + joined_shift
    grad_mixed = dot(upstream, dense_w, 1, 1).astype(BF)
    mixed, *grad_joined = attention(
        joined.reshape(2, length, 6 * HD),
        grad_mixed.reshape(2, length, 2 * HD),
        cos_table,
        sin_table,
        pos,
        doc,
    )
    mixed = mixed.reshape(2 * length, 2 * HD)
    grad_joined = jnp.concatenate(grad_joined, axis=-1).reshape(2 * length, 6 * HD)

    hidden = dot(normed_two, hidden_w, 1, 0) + hidden_shift
    below = 0.5 * (1.0 + lax.erf(hidden * (0.5**0.5)))
    active = (hidden * below).astype(BF)
    slope = below + hidden * jnp.exp(-0.5 * hidden * hidden) * ((2.0 * jnp.pi) ** (-0.5))
    grad_hidden = (dot(upstream, back_w, 1, 1) * slope).astype(BF)

    inner = jnp.concatenate([mixed, active], axis=1)
    out = dot(inner, jnp.concatenate([dense_w, back_w], axis=0), 1, 0).astype(BF)
    out = reduce_tokens(out, span)
    block_output = (own_in.astype(F32) + (out + (dense_shift + back_shift))).astype(BF)[None]

    grad_dense = reduce_dense(dot(mixed, upstream, 0, 0), copies)
    grad_back = dot(active, upstream, 0, 0).reshape(2, 1, copies, units, D)
    grad_back = reduce_replicas(grad_back, copies)[0]
    grad_tall = dot(normed_two, grad_hidden, 0, 0).reshape(2, 2, copies, 4 * rows, FF // 8)
    grad_tall = reduce_replicas(grad_tall, copies)
    grad_wide = dot(normed_one, grad_joined, 0, 0).reshape(2, 2, copies, 4 * rows, 6 * HD)
    grad_wide = reduce_replicas(grad_wide, copies)
    grads = jnp.concatenate([grad_wide, grad_tall], axis=2).astype(BF)
    grads = swap_shards(grads.reshape(8 * rows, -1)).astype(F32)
    grad_wide = grads[:, : 6 * HD].reshape(2, 2, 2, rows, 3, 2, HD)
    grad_wide = grad_wide.transpose(3, 4, 2, 0, 5, 1, 6).reshape(rows, 3 * D)
    grad_tall = grads[:, 6 * HD :].reshape(2, 2, 2, rows, 2, copies, units)
    grad_tall = grad_tall.transpose(3, 4, 0, 5, 1, 2, 6).reshape(rows, FF)

    grad_one = dot(grad_joined, joined_w, 1, 1)
    grad_two = dot(grad_hidden, hidden_w, 1, 1)
    pull = reduce_tokens((grad_one * gain_one + grad_two * gain_two).astype(BF), span)
    own_wide = own_in.astype(F32)
    own_centre = own_wide - jnp.mean(own_wide, axis=-1, keepdims=True)
    own_spread = lax.rsqrt(jnp.mean(own_centre * own_centre, axis=-1, keepdims=True) + EPS)
    own_normal = own_centre * own_spread
    pull = own_spread * (
        pull
        - jnp.mean(pull, axis=-1, keepdims=True)
        - own_normal * jnp.mean(pull * own_normal, axis=-1, keepdims=True)
    )
    grad_wide_own = own_grad.astype(F32)
    input_grad = (grad_wide_own + pull).astype(BF)[None]

    vectors = [
        jnp.sum(grad_one * normal, axis=0),
        jnp.sum(grad_one, axis=0),
        jnp.sum(grad_two * normal, axis=0),
        jnp.sum(grad_two, axis=0),
        jnp.sum(grad_wide_own, axis=0),
    ]
    joined_sum = jnp.sum(grad_joined.astype(F32), axis=0).reshape(3, 1, 1, 2, 1, HD)
    joined_sum = lax.dynamic_update_slice(
        jnp.zeros((3, 2, 2, 2, 2, HD), F32), joined_sum, (0, core, zl, 0, x, 0)
    )
    hidden_sum = jnp.sum(grad_hidden.astype(F32), axis=0).reshape(2, 1, copies, 1, 1, units)
    hidden_sum = lax.dynamic_update_slice(
        jnp.zeros((2, 2, copies, 2, 2, units), F32), hidden_sum, (0, zl, 0, x, core, 0)
    )
    sums = [v.reshape(count, -1) for v in (*vectors, joined_sum, hidden_sum)]
    sums = reduce_small(jnp.concatenate(sums, axis=1), copies)
    cut = lambda a, n: sums[a : a + n]
    bias_sum = cut(4 * rows, rows)

    return (
        block_output,
        input_grad,
        cut(0, rows),
        cut(rows, rows),
        grad_wide,
        cut(5 * rows, 3 * rows),
        grad_dense,
        bias_sum,
        cut(2 * rows, rows),
        cut(3 * rows, rows),
        grad_tall,
        cut(8 * rows, units),
        grad_back,
        bias_sum,
    )


def solution(mesh):
    copies = mesh.shape["batch"] // 4
    inner = Mesh(mesh.devices.reshape(2, 2, copies, 2, 2), AXES)
    batch, ctx = AXES[:3], AXES[3:]
    tokens = P(batch, ctx, None)
    vector, matrix = P(AXES), P(AXES, None)
    params = (vector, vector, matrix, vector, matrix, vector) * 1
    params = params + (vector, vector, matrix, vector, matrix, vector)
    return jax.shard_map(
        functools.partial(shards, copies),
        mesh=inner,
        in_specs=(tokens, tokens, P(batch, None), P(batch, None)) + params,
        out_specs=(tokens, tokens) + params,
        check_vma=False,
    )
```

```python
import functools

import jax
import jax.numpy as jnp
from jax import lax
from jax.experimental import pallas as pl
from jax.experimental.pallas import tpu as pltpu
from jax.sharding import Mesh, PartitionSpec as P

D = 2048
H = 16
HD = 128
ROT = 32
FF = 8192
WIDE = 6 * HD
UNITS = FF // 8
BLK = 256
NBLK = D // BLK
EPS = 1e-05
NEG = -1e30
THETA = 10000.0
BF = jnp.bfloat16
F32 = jnp.float32
AXES = ("zh", "zl", "y", "x", "core")
VMEM = 50 * 2**20
COST = 1.0


LINE = {}
DEPTH = {"core": 4}


def after(v, *others):
    return lax.optimization_barrier((v, *others))[0]


def queue(channel, v, step):
    line = LINE.setdefault(channel, [])
    depth = DEPTH.get(channel, 1)
    if len(line) >= depth:
        v = after(v, line[-depth])
    out = step(v)
    line.append(out[0] if isinstance(out, (list, tuple)) else out)
    return out


def flip(v, axis, channel=None):
    return queue(channel or axis, v, lambda w: lax.ppermute(w, axis, [(0, 1), (1, 0)]))


def dot(a, b, ca, cb):
    return lax.dot_general(a, b, (((ca,), (cb,)), ((), ())), preferred_element_type=F32)


def call(kernel, grid, ins, outs, shapes, scratch=(), flops=0, traffic=0, special=0, scalars=1):
    return pl.pallas_call(
        kernel,
        grid_spec=pltpu.PrefetchScalarGridSpec(
            num_scalar_prefetch=scalars,
            grid=grid,
            in_specs=ins,
            out_specs=outs,
            scratch_shapes=scratch,
        ),
        out_shape=shapes,
        compiler_params=pltpu.CompilerParams(vmem_limit_bytes=VMEM),
        cost_estimate=pl.CostEstimate(
            flops=int(flops * COST), bytes_accessed=int(traffic * COST), transcendentals=int(special * COST)
        ),
    )


def shape(*dims, dtype=BF):
    return jax.ShapeDtypeStruct(dims, dtype)


def fixed(*dims):
    return pl.BlockSpec(dims, lambda *_: (0,) * len(dims))


def rows_of(width, rows=BLK):
    return pl.BlockSpec((rows, width), lambda i, *_: (i, 0))


def two_halves(width):
    return [
        pl.BlockSpec((BLK, width), lambda i, *_: (jnp.minimum(i, 3), 0)),
        pl.BlockSpec((BLK, width), lambda i, *_: (jnp.maximum(i - 4, 0), 0)),
    ]


def pick(near, far):
    return jnp.where(pl.program_id(0) < 4, near[...], far[...])


def place(base, r, p):
    s = r ^ base
    return (s // 2) * 4 + p * 2 + s % 2


def columns(index):
    return pl.ds(pl.multiple_of(index * BLK, BLK), BLK)


def norm_kernel(near, far, gains, one, two, mean, scale):
    v = pick(near, far).astype(F32)
    mu = jnp.mean(v, axis=-1, keepdims=True)
    v = v - mu
    r = lax.rsqrt(jnp.mean(v * v, axis=-1, keepdims=True) + EPS)
    v = v * r
    one[...] = (v * gains[0:1] + gains[1:2]).astype(BF)
    two[...] = (v * gains[2:3] + gains[3:4]).astype(BF)
    mean[...] = mu
    scale[...] = r


def norms(near, far, gains):
    n = 2 * near.shape[0]
    return call(
        norm_kernel,
        (n // BLK,),
        [*two_halves(D), fixed(4, D)],
        [rows_of(D), rows_of(D), rows_of(1), rows_of(1)],
        [shape(n, D), shape(n, D), shape(n, 1, dtype=F32), shape(n, 1, dtype=F32)],
        traffic=n * D * 6,
        flops=n * D * 10,
        scalars=0,
    )(near, far, gains)


def joined_kernel(base, v, w0, w1, w2, w3, shift, out):
    total = jnp.zeros((BLK, WIDE), F32) + shift[...]
    for r, w in enumerate((w0, w1, w2, w3)):
        for p in range(2):
            total += dot(v[:, columns(place(base[0], r, p))], w[p], 1, 0)
    out[...] = total


def joined_product(base, v, pieces, shift):
    n = v.shape[0]
    return call(
        joined_kernel,
        (n // BLK,),
        [rows_of(D), *[fixed(2, BLK, WIDE)] * 4, fixed(1, WIDE)],
        rows_of(WIDE),
        shape(n, WIDE, dtype=F32),
        flops=2 * n * D * WIDE,
        traffic=n * D * 2 + n * WIDE * 4 + D * WIDE * 2,
    )(base, v, *pieces, shift)


def mixed_grad_kernel(near, far, w, out):
    out[...] = dot(pick(near, far), w[...], 1, 1).astype(BF)


def mixed_grad(near, far, w):
    n, wide = 2 * near.shape[0], w.shape[0]
    return call(
        mixed_grad_kernel,
        (n // BLK,),
        [*two_halves(D), fixed(wide, D)],
        rows_of(wide),
        shape(n, wide),
        flops=2 * n * D * wide,
        traffic=n * D * 2,
        scalars=0,
    )(near, far, w)


def hidden_kernel(
    skip, base, v, near, far, w0, w1, w2, w3, b0, b1, b2, b3, shift, active, grad, sums, back
):
    up = pick(near, far)
    for r, w in enumerate((b0, b1, b2, b3)):
        back[:, columns(r ^ base[0])] = dot(up, w[skip:], 1, 1)
    u = jnp.zeros((BLK, UNITS), F32) + shift[...]
    for r, w in enumerate((w0, w1, w2, w3)):
        for p in range(2):
            u += dot(v[:, columns(place(base[0], r, p))], w[p], 1, 0)
    below = 0.5 * (1.0 + lax.erf(u * (0.5**0.5)))
    active[...] = (u * below).astype(BF)
    slope = below + u * jnp.exp(-0.5 * u * u) * ((2.0 * jnp.pi) ** (-0.5))
    low = (back[...] * slope).astype(BF)
    grad[...] = low

    @pl.when(pl.program_id(0) == 0)
    def _():
        sums[...] = jnp.zeros_like(sums)

    sums[...] += jnp.sum(low.astype(F32), axis=0, keepdims=True)


def hidden_products(base, v, near, far, pieces, back_pieces, shift):
    n, tall = v.shape[0], back_pieces[0].shape[0]
    return call(
        functools.partial(hidden_kernel, tall - BLK),
        (n // BLK,),
        [rows_of(D), *two_halves(D), *[fixed(2, BLK, UNITS)] * 4, *[fixed(tall, D)] * 4, fixed(1, UNITS)],
        [rows_of(UNITS), rows_of(UNITS), fixed(1, UNITS)],
        [shape(n, UNITS), shape(n, UNITS), shape(1, UNITS, dtype=F32)],
        [pltpu.VMEM((BLK, UNITS), F32)],
        flops=4 * n * D * UNITS,
        traffic=n * D * 4 + n * UNITS * 4 + D * UNITS * 4,
        special=2 * n * UNITS,
    )(base, v, near, far, *pieces, *back_pieces, shift)


def out_kernel(skip, base, mixed, active, w, b0, b1, b2, b3, out):
    total = dot(mixed[...], w[...], 1, 0)
    for r, b in enumerate((b0, b1, b2, b3)):
        total += dot(active[:, columns(r ^ base[0])], b[skip:], 1, 0)
    out[...] = total.astype(BF)


def out_product(base, half, mixed, active, dense_w, back_pieces):
    n, tall = mixed.shape[0] // 2, back_pieces[0].shape[0]
    steps = n // BLK
    half_rows = lambda width: pl.BlockSpec((BLK, width), lambda i, *_: (i + half * steps, 0))
    return call(
        functools.partial(out_kernel, tall - BLK),
        (steps,),
        [half_rows(2 * HD), half_rows(UNITS), fixed(2 * HD, D), *[fixed(tall, D)] * 4],
        rows_of(D),
        shape(n, D),
        flops=2 * n * D * (UNITS + 2 * HD),
        traffic=n * D * 2 + n * UNITS * 2 + D * UNITS * 2,
    )(base, mixed, active, dense_w, *back_pieces)


def pull_kernel(
    base, dq, dk, dv, du, tokens, mean, scale, gains, q0, q1, q2, q3, w0, w1, w2, w3, out, sums, wide
):
    @pl.when(pl.program_id(0) == 0)
    def _():
        sums[...] = jnp.zeros_like(sums)
        wide[...] = jnp.zeros_like(wide)

    add = lambda v: jnp.sum(v, axis=0, keepdims=True)
    for t, v in enumerate((dq, dk, dv)):
        wide[:, 2 * HD * t : 2 * HD * (t + 1)] += add(v[...].astype(F32))
    for r, (q, w) in enumerate(((q0, w0), (q1, w1), (q2, w2), (q3, w3))):
        for p in range(2):
            at = columns(place(base[0], r, p))
            one = (
                dot(dq[...], q[p, :, 0 : 2 * HD], 1, 1)
                + dot(dk[...], q[p, :, 2 * HD : 4 * HD], 1, 1)
                + dot(dv[...], q[p, :, 4 * HD :], 1, 1)
            )
            two = dot(du[...], w[p], 1, 1)
            normal = (tokens[:, at].astype(F32) - mean[...]) * scale[...]
            sums[0:1, at] += add(one * normal)
            sums[1:2, at] += add(one)
            sums[2:3, at] += add(two * normal)
            sums[3:4, at] += add(two)
            out[:, at] = (one * gains[0:1, at] + two * gains[2:3, at]).astype(BF)


def pull_product(base, half, grads, du, tokens, mean, scale, gains, joined_pieces, pieces):
    n = du.shape[0] // 2
    steps = n // BLK
    half_rows = lambda width: pl.BlockSpec((BLK, width), lambda i, *_: (i + half * steps, 0))
    return call(
        pull_kernel,
        (steps,),
        [
            *[half_rows(2 * HD)] * 3,
            half_rows(UNITS),
            rows_of(D),
            half_rows(1),
            half_rows(1),
            fixed(4, D),
            *[fixed(2, BLK, WIDE)] * 4,
            *[fixed(2, BLK, UNITS)] * 4,
        ],
        [rows_of(D), fixed(4, D), fixed(1, WIDE)],
        [shape(n, D), shape(4, D, dtype=F32), shape(1, WIDE, dtype=F32)],
        flops=2 * n * D * (UNITS + WIDE),
        traffic=n * D * 4 + n * UNITS * 4 + D * (UNITS + WIDE) * 2,
    )(base, *grads, du, tokens, mean, scale, gains, *joined_pieces, *pieces)


def rows_grad_kernel(count, base, v, *refs):
    rights, outs = refs[:count], refs[count:]
    step = pl.program_id(0)
    v = v[...]
    parts, width = [], 0
    for right in rights:
        parts.append(dot(v, right[...], 0, 0).astype(BF))
    for j, out in enumerate(outs):

        @pl.when(step // 2 == j)
        def _(out=out):
            at = 0
            for part in parts:
                out[:, at : at + part.shape[1]] = part
                at += part.shape[1]


def rows_grad(base, v, rights, order):
    n, width = v.shape[0], sum(r.shape[1] for r in rights)

    def chosen(i, b):
        r = sum(jnp.where(i // 2 == j, r, 0) for j, r in enumerate(order))
        return (0, place(b[0], r, i % 2))

    def slot(j):
        return pl.BlockSpec((BLK, width), lambda i, b: (jnp.clip(i - 2 * j, 0, 1), 0))

    return call(
        functools.partial(rows_grad_kernel, len(rights)),
        (2 * len(order),),
        [pl.BlockSpec((n, BLK), chosen), *[fixed(*r.shape) for r in rights]],
        [slot(j) for j in range(len(order))],
        [shape(2 * BLK, width)] * len(order),
        flops=2 * n * BLK * 2 * len(order) * width,
        traffic=n * width * 2 + n * BLK * 4 * len(order),
    )(base, v, *rights)


def units_grad_kernel(base, v, near, far, *outs):
    step, n = pl.program_id(0), near.shape[0]
    part = dot(v[:n], near[...], 0, 0) + dot(v[n:], far[...], 0, 0)
    part = part.astype(BF)
    for j, out in enumerate(outs):

        @pl.when(step == j)
        def _(out=out):
            out[...] = part


def units_grad(base, v, near, far, order):
    n = v.shape[0]

    def chosen(i, b):
        return (0, sum(jnp.where(i == j, r, 0) for j, r in enumerate(order)) ^ b[0])

    return call(
        units_grad_kernel,
        (len(order),),
        [pl.BlockSpec((n, BLK), chosen), fixed(n // 2, D), fixed(n // 2, D)],
        [fixed(BLK, D)] * len(order),
        [shape(BLK, D)] * len(order),
        flops=2 * n * BLK * D * len(order),
        traffic=n * D * 2 + (n + D) * BLK * 2 * len(order),
    )(base, v, near, far)


def turn(v, cos, sin):
    lane = lax.broadcasted_iota(jnp.int32, v.shape, 1)
    half = ROT // 2
    swapped = jnp.where(lane < half, pltpu.roll(v, HD - half, 1), pltpu.roll(v, half, 1))
    return v * cos + swapped * sin


def attention_kernel(
    q, k, v, do, cq, sq, ck, sk, pq, eq, pk, ek, o, dq, dk, dv, ks, vs, dka, dva
):
    i = pl.program_id(2)
    scale = HD ** (-0.5)
    flat = lambda a: a.reshape(-1, HD)

    @pl.when(i == 0)
    def _():
        ks[...] = turn(flat(k[...]), ck[...], sk[...]).astype(BF)
        vs[...] = flat(v[...]).astype(BF)
        dka[...] = jnp.zeros_like(dka)
        dva[...] = jnp.zeros_like(dva)

    qr = turn(q[...], cq[...], sq[...]).astype(BF)
    s = dot(qr, ks[...], 1, 1) * scale
    allowed = (pk[...] <= pq[...]) & (ek[...] == eq[...])
    s = jnp.where(allowed, s, NEG)
    e = jnp.exp(s - jnp.max(s, axis=-1, keepdims=True))
    p = e / jnp.sum(e, axis=-1, keepdims=True)
    low = p.astype(BF)
    o[...] = dot(low, vs[...], 1, 0).astype(BF)
    dp = dot(do[...], vs[...], 1, 1)
    ds = (p * (dp - jnp.sum(p * dp, axis=-1, keepdims=True))).astype(BF)
    dq[...] = turn(dot(ds, ks[...], 1, 0) * scale, cq[...], -sq[...]).astype(BF)
    dva[...] += dot(low, do[...], 0, 0)
    dka[...] += dot(ds, qr, 0, 0)

    @pl.when(i == pl.num_programs(2) - 1)
    def _():
        dk[...] = turn(dka[...] * scale, ck[...], -sk[...]).astype(BF).reshape(dk.shape)
        dv[...] = dva[...].astype(BF).reshape(dv.shape)


def attention(joined, grad, cos, sin, pos, doc):
    half = 2 * BLK
    length = 2 * half
    joined = joined.reshape(2, 2, half, WIDE)
    grad = grad.reshape(2, 2, half, 2 * HD)
    part = lambda off: pl.BlockSpec(
        (None, None, BLK, HD), lambda s, h, i: (i // 2, s, i % 2, off + h)
    )
    whole = lambda off: pl.BlockSpec((2, None, half, HD), lambda s, h, i: (0, s, 0, off + h))
    tq = pl.BlockSpec((None, BLK, HD), lambda s, h, i: (s, i, 0))
    tk = pl.BlockSpec((None, length, HD), lambda s, h, i: (s, 0, 0))
    col = pl.BlockSpec((None, BLK, 1), lambda s, h, i: (s, i, 0))
    row = pl.BlockSpec((None, 1, length), lambda s, h, i: (s, 0, 0))
    results = call(
        attention_kernel,
        (2, 2, length // BLK),
        [part(0), whole(2), whole(4), part(0), tq, tq, tk, tk, col, col, row, row],
        [part(0), part(0), whole(0), whole(0)],
        [shape(2, 2, half, 2 * HD)] * 4,
        [
            pltpu.VMEM((length, HD), BF),
            pltpu.VMEM((length, HD), BF),
            pltpu.VMEM((length, HD), F32),
            pltpu.VMEM((length, HD), F32),
        ],
        flops=4 * length * length * HD * 14,
        traffic=4 * length * HD * 24,
        special=4 * length * length,
        scalars=0,
    )(
        joined, joined, joined, grad, cos, sin, cos, sin,
        pos[:, :, None], doc[:, :, None], pos[:, None, :], doc[:, None, :],
    )
    return [r.reshape(2 * length, 2 * HD) for r in results]


def column_plan(copies):
    units = FF // (16 * copies)
    for d in range(8):
        zl, x, core = d // 4, d // 2 % 2, d % 2
        for t in range(3):
            for m in range(2):
                head = core * 8 + zl * 4 + m * 2 + x
                yield 0, t * D + head * HD, HD, d, (t * 2 + m) * HD
        for zh in range(2):
            for y in range(copies):
                owner = (((zh * 2 + zl) * copies + y) * 2 + x) * 2 + core
                yield 1, owner * units, units, d, (zh * copies + y) * units


def deal_kernel(copies, wide, tall, wide_out, tall_out):
    pairs = ((wide, wide_out), (tall, tall_out))
    for which, start, width, d, at in column_plan(copies):
        source, target = pairs[which]
        target[d, :, at : at + width] = source[:, start : start + width]


def deal_columns(wide, tall, copies):
    rows = wide.shape[0]
    return call(
        functools.partial(deal_kernel, copies),
        (1,),
        [fixed(*wide.shape), fixed(*tall.shape)],
        [fixed(8, rows, WIDE), fixed(8, rows, UNITS)],
        [shape(8, rows, WIDE), shape(8, rows, UNITS)],
        traffic=rows * (3 * D + FF) * 4,
        scalars=0,
    )(wide, tall)


def collect_kernel(copies, which_one, source, target):
    for which, start, width, d, at in column_plan(copies):
        if which == which_one:
            target[:, start : start + width] = source[d, :, at : at + width].astype(F32)


def collect_columns(v, which, copies):
    rows, width = v.shape[1], (3 * D, FF)[which]
    return call(
        functools.partial(collect_kernel, copies, which),
        (1,),
        [fixed(*v.shape)],
        fixed(rows, width),
        shape(rows, width, dtype=F32),
        traffic=rows * width * 6,
        scalars=0,
    )(v)


def pack_kernel(*refs):
    for j, v in enumerate(refs[:-1]):
        refs[-1][j : j + 1, 0 : v.shape[1]] = v[...]


def pack_rows(vectors):
    vectors = [v[None] for v in vectors]
    return call(
        pack_kernel,
        (1,),
        [fixed(*v.shape) for v in vectors],
        fixed(len(vectors), BLK),
        shape(len(vectors), BLK),
        scalars=0,
    )(*vectors)


def swap(v, axes=("zl", "x", "core")):
    return queue("swap", v, lambda w: lax.all_to_all(w, axes, 0, 0, tiled=True))


def gather_plain(v, split):
    return split(lax.all_gather(v, ("zh", "y"), axis=0, tiled=False))


def half_sum(v, other):
    return (v.astype(F32) + other.astype(F32)).astype(BF)


def split_rows(copies):
    def split(w):
        c = w.shape[-1]
        w = w.reshape(2, copies, 2, -1, c).transpose(0, 2, 1, 3, 4).reshape(2, 2, 2, BLK, c)
        return [w[a, :, b] for a in (0, 1) for b in (0, 1)]

    return split


def join_rows(copies):
    def join(w):
        c = w.shape[-1]
        w = w.reshape(2, 2, 2, BLK, c).transpose(0, 2, 1, 3, 4)
        w = w.reshape(2, 2, copies, -1, c).transpose(0, 2, 1, 3, 4)
        return w.reshape(2 * copies, -1, c)

    return join


def reduce_tokens(near, far, span):
    block = lambda v, f: v[f * span : (f + 1) * span]
    got = {f: flip(block(far, f), "core") for f in (3, 1, 2, 0)}
    total = lambda f: block(near, f).astype(F32) + got[f].astype(F32)
    away_x = flip(total(3).astype(BF), "x")
    mine_x = flip(total(1).astype(BF), "x")
    from_far = flip((total(2) + away_x.astype(F32)).astype(BF), "zl")
    return total(0) + mine_x.astype(F32) + from_far.astype(F32)


def flip_parts(v, axis, parts=2, cut=0):
    size = v.shape[cut] // parts
    pieces = [lax.slice_in_dim(v, j * size, (j + 1) * size, axis=cut) for j in range(parts)]
    return [flip(p, axis) for p in pieces]


def dense_rows(pieces):
    core = lax.axis_index("core")
    zh, y = lax.axis_index("zh"), lax.axis_index("y")
    first = core == 0
    w = jnp.stack(pieces).reshape(2, 2, HD // 2, D)
    w = jnp.where(y == 0, w, w[:, ::-1])
    same = zh == core
    keep, send = jnp.where(same, w[0], w[1]), jnp.where(same, w[1], w[0])
    other = flip(send, "core")
    low, high = jnp.where(first, keep, other), jnp.where(first, other, keep)
    return jnp.stack([low, high], axis=1).reshape(2 * HD, D)


def gather_dense_plain(w):
    core, x = lax.axis_index("core"), lax.axis_index("x")
    w = lax.all_gather(w, ("zh", "y", "x", "core"), axis=0, tiled=True).reshape(2, 2, 2, HD, D)
    w = lax.dynamic_slice(w, (core, 0, x, 0, 0), (1, 2, 1, HD, D))
    return w.reshape(2 * HD, D)


def reduce_dense(g, copies):
    core, x = lax.axis_index("core"), lax.axis_index("x")
    if copies != 2:
        w = jnp.zeros((2, 2, 2, HD, D), F32)
        g = g.astype(F32).reshape(1, 2, 1, HD, D)
        w = lax.dynamic_update_slice(w, g, (core, 0, x, 0, 0)).reshape(-1, D)
        return lax.psum_scatter(w, ("zh", "y", "x", "core"), scatter_dimension=0, tiled=True)
    zh, y = lax.axis_index("zh"), lax.axis_index("y")
    g = g.reshape(2, 2, HD // 2, D)
    first, same = core == 0, zh == core
    keep = jnp.where(first, g[:, 0], g[:, 1])
    other = flip(jnp.where(first, g[:, 1], g[:, 0]), "core")
    w = jnp.stack([jnp.where(same, keep, other), jnp.where(same, other, keep)])
    w = jnp.where(y == 0, w, w[:, ::-1])
    w = w[:, 0].astype(F32) + flip(w[:, 1], "y").astype(F32)
    return w[0] + flip(w[1].astype(BF), "zh").astype(F32)


def shards(
    copies,
    block_input,
    output_grad,
    documents,
    span_order,
    attention_norm_gain,
    attention_norm_bias,
    query_key_value_weight,
    query_key_value_bias,
    dense_weight,
    dense_bias,
    mlp_norm_gain,
    mlp_norm_bias,
    to_hidden_weight,
    to_hidden_bias,
    from_hidden_weight,
    from_hidden_bias,
):
    LINE.clear()
    span = block_input.shape[1]
    count = 16 * copies
    rows = D // count
    units = FF // count
    length = 4 * span
    zl, x, core = (lax.axis_index(a) for a in ("zl", "x", "core"))
    own_in, own_grad = block_input[0], output_grad[0]
    kernel = lambda v, step, *first: queue("kernel", after(v, *first) if first else v, step)
    base = jnp.zeros((1,), jnp.int32)
    if copies == 2:
        base = base + lax.axis_index("zh") * 2 + lax.axis_index("y")

    vectors = (
        attention_norm_gain,
        attention_norm_bias,
        mlp_norm_gain,
        mlp_norm_bias,
        dense_bias,
        from_hidden_bias,
        query_key_value_bias,
        to_hidden_bias,
    )
    if copies == 2:
        small = pack_rows(vectors)
    else:
        small = jnp.stack([jnp.pad(v, (0, BLK - v.shape[0])) for v in vectors])
    facts = jnp.concatenate([documents[0], jnp.pad(span_order[0], (0, length - 4))])
    small = jnp.concatenate([small, facts.astype(BF).reshape(8, BLK)], axis=0)
    small = jnp.broadcast_to(small[None], (count, 16, BLK)).reshape(count * 16, BLK)

    wide, tall = deal_columns(query_key_value_weight, to_hidden_weight, copies)
    wide = swap(wide).reshape(2, 4 * rows, WIDE)
    tall = swap(tall).reshape(2, 4 * rows, UNITS)
    small = swap(small, AXES).reshape(count, 16, BLK)
    in_zl, in_x = flip(own_in, "zl"), flip(own_in, "x")
    if copies == 2:
        chunk = jnp.concatenate([dense_weight, from_hidden_weight], axis=0)
        join = lambda v: jnp.concatenate(v, axis=0)
        back_near = flip(chunk, "y")
        back_far = flip_parts(chunk, "zh")
        wide_near = flip(wide, "y")
        wide_far = flip(wide, "zh")
        tall_near = flip(tall, "y")
        tall_far = flip_parts(tall, "zh")
        back_both = flip(join(back_far), "y")
        wide_pieces = [wide, wide_near, wide_far, flip(wide_far, "y")]
        tall_both = [flip(v, "y") for v in tall_far]
        tall_pieces = [tall, tall_near, join(tall_far), join(tall_both)]
        back_pieces = [chunk, back_near, join(back_far), back_both]
    in_both = flip(in_zl, "x")
    other_core = lambda blocks: jnp.concatenate([flip(v, "core") for v in blocks], axis=0)
    near = [own_in, in_x, in_zl, in_both]
    far = other_core(near)
    near = jnp.concatenate(near, axis=0)
    up_zl, up_x = flip(own_grad, "zl"), own_grad
    if copies == 2:
        up_x = after(up_x, back_far[1])
    up_x = flip(up_x, "x")
    if copies == 2:
        up_zl = after(up_zl, wide_far, tall_near)
    up_both = flip(up_zl, "x")
    near_up = [own_grad, up_x, up_zl, up_both]
    far_up = other_core(near_up)
    near_up = jnp.concatenate(near_up, axis=0)
    if copies == 2:
        dense_w = dense_rows([p[:rows] for p in back_pieces])
    else:
        wide_pieces = gather_plain(wide, split_rows(copies))
        tall_pieces = gather_plain(tall, split_rows(copies))
        back_pieces = gather_plain(from_hidden_weight, lambda w: list(w.reshape(4, BLK, D)))
        dense_w = gather_dense_plain(dense_weight)

    row = (lax.axis_index("zh") * 2 * copies + lax.axis_index("y")) * 4
    facts = [lax.dynamic_slice(small, (row + s * copies * 4, 8, 0), (1, 8, BLK)) for s in (zl, 1 - zl)]
    facts = [v.astype(jnp.int32).reshape(2 * length) for v in facts]
    small = small[:, :8].astype(F32)
    take = lambda j, n: small[:, j, :n].reshape(-1)
    gains = jnp.stack([take(j, rows) for j in range(4)])
    out_shift = take(4, rows) + take(5, rows)
    joined_shift = take(6, 3 * rows).reshape(3, 2, 2, 2, 2, HD)
    joined_shift = lax.dynamic_slice(joined_shift, (0, core, zl, 0, x, 0), (3, 1, 1, 2, 1, HD))
    joined_shift = joined_shift.reshape(1, WIDE)
    hidden_shift = take(7, units).reshape(2, 2, copies, 2, 2, units)
    hidden_shift = lax.dynamic_slice(
        hidden_shift, (0, zl, 0, x, core, 0), (2, 1, copies, 1, 1, units)
    ).reshape(1, UNITS)

    offsets = jnp.arange(span, dtype=jnp.int32)
    pos, doc = [], []
    for known in facts:
        for c in (0, 1):
            for b in (0, 1):
                block = (x ^ b) * 2 + (core ^ c)
                doc.append(lax.dynamic_slice(known, (block * span,), (span,)))
                pos.append(lax.dynamic_slice(known, (length + block,), (1,)) * span + offsets)
    pos = jnp.concatenate(pos).reshape(2, length)
    doc = jnp.concatenate(doc).reshape(2, length)
    inverse = jnp.power(THETA, -jnp.arange(ROT // 2, dtype=F32) * (2.0 / ROT))
    angles = pos.astype(F32)[:, :, None] * inverse
    cosine, sine = jnp.cos(angles), jnp.sin(angles)
    rest = jnp.zeros((2, length, HD - ROT), F32)
    cos_table = jnp.concatenate([cosine, cosine, rest + 1.0], axis=-1)
    sin_table = jnp.concatenate([-sine, sine, rest], axis=-1)

    order = (3, 1, 2, 0)
    ordered = lambda v: [v[order.index(r)] for r in range(4)]
    normed_one, normed_two, mean, scale = kernel(gains, lambda v: norms(near, far, v))
    grad_mixed = kernel(dense_w, lambda v: mixed_grad(near_up, far_up, v))
    joined = kernel(normed_one, lambda v: joined_product(base, v, wide_pieces, joined_shift))
    mixed, *grads = kernel(
        joined, lambda v: attention(v, grad_mixed, cos_table, sin_table, pos, doc)
    )
    pair = copies == 2
    ties = lambda *v: v if pair else ()
    far_half = lambda v: half_sum(v[2], flip(v[3], "y")) if pair else v[2]
    grad_wide = ordered(kernel(normed_one, lambda v: rows_grad(base, v, grads, order)))
    wide_far = far_half(grad_wide)
    half = mixed.shape[0] // 2
    grad_dense = dot(mixed[:half], near_up, 0, 0) + dot(mixed[half:], far_up, 0, 0)
    grad_dense = grad_dense.astype(BF)
    active, grad_hidden, hidden_sum = kernel(
        normed_two,
        lambda v: hidden_products(
            base, v, near_up, far_up, tall_pieces, back_pieces, hidden_shift
        ),
        grad_dense,
    )
    grad_tall = ordered(
        kernel(grad_hidden, lambda v: rows_grad(base, normed_two, [v], order), *ties(wide_far))
    )
    wide_sum = flip(wide_far, "zh") if pair else None
    tall_far = far_half(grad_tall)
    grad_back = ordered(kernel(active, lambda v: units_grad(base, v, near_up, far_up, order)))
    pull_half = lambda h, *first: kernel(
        grad_hidden,
        lambda v: pull_product(
            base, h, grads, v, far if h else near, mean, scale, gains, wide_pieces, tall_pieces
        ),
        *first,
    )
    out_half = lambda h, *first: kernel(
        mixed, lambda v: out_product(base, h, v, active, dense_w, back_pieces), *first
    )
    pull_far, pull_far_sums, pull_far_wide = pull_half(1, *ties(tall_far, wide_sum))
    back_far = far_half(grad_back)
    pull_near, pull_near_sums, pull_near_wide = pull_half(0)
    tall_sum = flip_parts(tall_far, "zh") if pair else ()
    out_far = out_half(1, *ties(back_far), *tall_sum[:1])
    out_near = out_half(0, *tall_sum[1:])
    tall_sum = jnp.concatenate(tall_sum) if pair else None
    pull = reduce_tokens(pull_near, pull_far, span)
    back_sum = jnp.concatenate(flip_parts(back_far, "zh")) if pair else None
    out = reduce_tokens(out_near, out_far, span)

    def near_half(v, far, join):
        if pair:
            return v[0].astype(F32) + flip(v[1], "y").astype(F32) + far.astype(F32)
        w = join(jnp.stack(v).astype(F32))
        return lax.psum_scatter(w, ("zh", "y"), scatter_dimension=0, tiled=False)

    own_wide = own_in.astype(F32)
    block_output = (own_wide + (out + out_shift)).astype(BF)[None]
    own_centre = own_wide - jnp.mean(own_wide, axis=-1, keepdims=True)
    own_spread = lax.rsqrt(jnp.mean(own_centre * own_centre, axis=-1, keepdims=True) + EPS)
    own_normal = own_centre * own_spread
    pull = own_spread * (
        pull
        - jnp.mean(pull, axis=-1, keepdims=True)
        - own_normal * jnp.mean(pull * own_normal, axis=-1, keepdims=True)
    )
    grad_own = own_grad.astype(F32)
    input_grad = (grad_own + pull).astype(BF)[None]

    vectors = pull_near_sums + pull_far_sums
    joined_sum = (pull_near_wide + pull_far_wide).reshape(3, 1, 1, 2, 1, HD)
    joined_sum = lax.dynamic_update_slice(
        jnp.zeros((3, 2, 2, 2, 2, HD), F32), joined_sum, (0, core, zl, 0, x, 0)
    )
    hidden_sum = lax.dynamic_update_slice(
        jnp.zeros((2, 2, copies, 2, 2, units), F32),
        hidden_sum.reshape(2, 1, copies, 1, 1, units),
        (0, zl, 0, x, core, 0),
    )
    sums = [*vectors, jnp.sum(grad_own, axis=0), joined_sum, hidden_sum]
    sums = jnp.concatenate([v.reshape(count, -1) for v in sums], axis=1)
    sums = jnp.sum(swap(sums, AXES), axis=0)
    cut = lambda a, n: sums[a : a + n]
    bias_sum = cut(4 * rows, rows)

    grad_wide = near_half(grad_wide, wide_sum, join_rows(copies)).astype(BF)
    grad_wide = collect_columns(swap(grad_wide.reshape(8, rows, WIDE)), 0, copies)
    grad_tall = near_half(grad_tall, tall_sum, join_rows(copies)).astype(BF)
    grad_tall = collect_columns(swap(grad_tall.reshape(8, rows, UNITS)), 1, copies)
    grad_dense = reduce_dense(grad_dense, copies)
    grad_back = near_half(grad_back, back_sum, lambda w: w.reshape(2 * copies, units, D))


    return (
        block_output,
        input_grad,
        cut(0, rows),
        cut(rows, rows),
        grad_wide,
        cut(5 * rows, 3 * rows),
        grad_dense,
        bias_sum,
        cut(2 * rows, rows),
        cut(3 * rows, rows),
        grad_tall,
        cut(8 * rows, units),
        grad_back,
        bias_sum,
    )


def solution(mesh):
    copies = mesh.shape["batch"] // 4
    inner = Mesh(mesh.devices.reshape(2, 2, copies, 2, 2), AXES)
    batch, ctx = AXES[:3], AXES[3:]
    tokens = P(batch, ctx, None)
    vector, matrix = P(AXES), P(AXES, None)
    params = (vector, vector, matrix, vector, matrix, vector)
    return jax.shard_map(
        functools.partial(shards, copies),
        mesh=inner,
        in_specs=(tokens, tokens, P(batch, None), P(batch, None)) + params + params,
        out_specs=(tokens, tokens) + params + params,
        check_vma=False,
    )
```

```python
import functools

import jax
import jax.numpy as jnp
from jax import lax
from jax.experimental import pallas as pl
from jax.experimental.pallas import tpu as pltpu
from jax.sharding import Mesh, PartitionSpec as P

D = 2048
H = 16
HD = 128
ROT = 32
FF = 8192
WIDE = 6 * HD
UNITS = FF // 8
BLK = 256
NBLK = D // BLK
EPS = 1e-05
NEG = -1e30
THETA = 10000.0
BF = jnp.bfloat16
F32 = jnp.float32
AXES = ("zh", "zl", "y", "x", "core")
VMEM = 50 * 2**20
COST = 1.0


CFG = {
    "swap": ["sw", "st", "ss", "gw", "gt", "gs"],
    "kernel": ["deal", "norms", "joined", "dO", "A", "W", "H", "T", "Pf", "Pn", "B", "Of", "On"],
    "x": ["ix", "ib", "ux", "ub", "p3", "p1", "o3", "o1"],
    "zl": ["iz", "uz", "pz", "oz"],
    "core": ["i0", "i1", "i2", "i3", "u0", "u1", "u2", "u3", "dc", "gd", "pc3", "pc1", "pc2", "pc0", "oc3", "oc1", "oc2", "oc0"],
    "y": ["An", "Wn", "Af0", "Wf", "Af1", "W3", "T3", "W1", "D1", "T1"],
    "zh": ["A0z", "Wz", "A1z", "zW", "zT0", "zT1", "zD"],
    "sc": ["Tg", "Br"],
    "depth": {"core": 3},
    "ties": {
        "T": ["W3"],
        "Pn": ["zW", "T3"],
        "B": ["zT0"],
        "o1": ["zT1", "T1"],
        "oz": ["gt"],
    },
}


def after(v, *others):
    return lax.optimization_barrier((v, *others))[0]


def flip(v, axis):
    return lax.ppermute(v, axis, [(0, 1), (1, 0)])


def run(tasks, skip=()):
    channels = ("swap", "kernel", "x", "zl", "core", "y", "zh", "sc")
    lines = {c: [n for n in CFG[c] if n not in skip] for c in channels}
    done, at = {}, dict.fromkeys(lines, 0)
    first = lambda v: v[0] if isinstance(v, (list, tuple)) else v
    while any(at[c] < len(lines[c]) for c in lines):
        moved = False
        for c, names in lines.items():
            while at[c] < len(names):
                name = names[at[c]]
                source, step = tasks[name]
                waits = [w for w in CFG["ties"].get(name, ()) if w not in skip]
                place = at[c] - CFG["depth"].get(c, 1)
                if place >= 0:
                    waits.append(names[place])
                if any(w not in done for w in waits):
                    break
                try:
                    v = source(done)
                    if waits:
                        v = after(v, *[first(done[w]) for w in waits])
                    done[name] = step(v, done)
                except KeyError:
                    break
                at[c] += 1
                moved = True
        assert moved
    return done


def dot(a, b, ca, cb):
    return lax.dot_general(a, b, (((ca,), (cb,)), ((), ())), preferred_element_type=F32)


def call(kernel, grid, ins, outs, shapes, scratch=(), flops=0, traffic=0, special=0, scalars=1):
    return pl.pallas_call(
        kernel,
        grid_spec=pltpu.PrefetchScalarGridSpec(
            num_scalar_prefetch=scalars,
            grid=grid,
            in_specs=ins,
            out_specs=outs,
            scratch_shapes=scratch,
        ),
        out_shape=shapes,
        compiler_params=pltpu.CompilerParams(vmem_limit_bytes=VMEM),
        cost_estimate=pl.CostEstimate(
            flops=int(flops * COST), bytes_accessed=int(traffic * COST), transcendentals=int(special * COST)
        ),
    )


def shape(*dims, dtype=BF):
    return jax.ShapeDtypeStruct(dims, dtype)


def fixed(*dims):
    return pl.BlockSpec(dims, lambda *_: (0,) * len(dims))


def rows_of(width, rows=BLK):
    return pl.BlockSpec((rows, width), lambda i, *_: (i, 0))


def two_halves(width):
    return [
        pl.BlockSpec((BLK, width), lambda i, *_: (jnp.minimum(i, 3), 0)),
        pl.BlockSpec((BLK, width), lambda i, *_: (jnp.maximum(i - 4, 0), 0)),
    ]


def pick(near, far):
    return jnp.where(pl.program_id(0) < 4, near[...], far[...])


def place(base, r, p):
    s = r ^ base
    return (s // 2) * 4 + p * 2 + s % 2


def columns(index):
    return pl.ds(pl.multiple_of(index * BLK, BLK), BLK)


def norm_kernel(near, far, gains, one, two, mean, scale):
    v = pick(near, far).astype(F32)
    mu = jnp.mean(v, axis=-1, keepdims=True)
    v = v - mu
    r = lax.rsqrt(jnp.mean(v * v, axis=-1, keepdims=True) + EPS)
    v = v * r
    one[...] = (v * gains[0:1] + gains[1:2]).astype(BF)
    two[...] = (v * gains[2:3] + gains[3:4]).astype(BF)
    mean[...] = mu
    scale[...] = r


def norms(near, far, gains):
    n = 2 * near.shape[0]
    return call(
        norm_kernel,
        (n // BLK,),
        [*two_halves(D), fixed(4, D)],
        [rows_of(D), rows_of(D), rows_of(1), rows_of(1)],
        [shape(n, D), shape(n, D), shape(n, 1, dtype=F32), shape(n, 1, dtype=F32)],
        traffic=n * D * 6,
        flops=n * D * 10,
        scalars=0,
    )(near, far, gains)


def joined_kernel(base, v, w0, w1, w2, w3, shift, out):
    total = jnp.zeros((BLK, WIDE), F32) + shift[...]
    for r, w in enumerate((w0, w1, w2, w3)):
        for p in range(2):
            total += dot(v[:, columns(place(base[0], r, p))], w[p], 1, 0)
    out[...] = total


def joined_product(base, v, pieces, shift):
    n = v.shape[0]
    return call(
        joined_kernel,
        (n // BLK,),
        [rows_of(D), *[fixed(2, BLK, WIDE)] * 4, fixed(1, WIDE)],
        rows_of(WIDE),
        shape(n, WIDE, dtype=F32),
        flops=2 * n * D * WIDE,
        traffic=n * D * 2 + n * WIDE * 4 + D * WIDE * 2,
    )(base, v, *pieces, shift)


def mixed_grad_kernel(near, far, w, out):
    out[...] = dot(pick(near, far), w[...], 1, 1).astype(BF)


def mixed_grad(near, far, w):
    n, wide = 2 * near.shape[0], w.shape[0]
    return call(
        mixed_grad_kernel,
        (n // BLK,),
        [*two_halves(D), fixed(wide, D)],
        rows_of(wide),
        shape(n, wide),
        flops=2 * n * D * wide,
        traffic=n * D * 2,
        scalars=0,
    )(near, far, w)


def hidden_kernel(
    skip, base, v, near, far, w, b0, b1, b2, b3, shift, active, grad, sums, back
):
    up = pick(near, far)
    for r, b in enumerate((b0, b1, b2, b3)):
        back[:, columns(r ^ base[0])] = dot(up, b[skip:], 1, 1)
    u = jnp.zeros((BLK, UNITS), F32) + shift[...]
    for r in range(4):
        for p in range(2):
            u += dot(v[:, columns(place(base[1], r, p))], w[r, p], 1, 0)
    below = 0.5 * (1.0 + lax.erf(u * (0.5**0.5)))
    active[...] = (u * below).astype(BF)
    slope = below + u * jnp.exp(-0.5 * u * u) * ((2.0 * jnp.pi) ** (-0.5))
    low = (back[...] * slope).astype(BF)
    grad[...] = low

    @pl.when(pl.program_id(0) == 0)
    def _():
        sums[...] = jnp.zeros_like(sums)

    sums[...] += jnp.sum(low.astype(F32), axis=0, keepdims=True)


def hidden_products(base, v, near, far, pieces, back_pieces, shift):
    n, tall = v.shape[0], back_pieces[0].shape[0]
    return call(
        functools.partial(hidden_kernel, tall - BLK),
        (n // BLK,),
        [rows_of(D), *two_halves(D), fixed(4, 2, BLK, UNITS), *[fixed(tall, D)] * 4, fixed(1, UNITS)],
        [rows_of(UNITS), rows_of(UNITS), fixed(1, UNITS)],
        [shape(n, UNITS), shape(n, UNITS), shape(1, UNITS, dtype=F32)],
        [pltpu.VMEM((BLK, UNITS), F32)],
        flops=4 * n * D * UNITS,
        traffic=n * D * 4 + n * UNITS * 4 + D * UNITS * 4,
        special=2 * n * UNITS,
    )(base, v, near, far, pieces, *back_pieces, shift)


def out_kernel(skip, base, mixed, active, w, b0, b1, b2, b3, out):
    total = dot(mixed[...], w[...], 1, 0)
    for r, b in enumerate((b0, b1, b2, b3)):
        total += dot(active[:, columns(r ^ base[0])], b[skip:], 1, 0)
    out[...] = total.astype(BF)


def out_product(base, half, mixed, active, dense_w, back_pieces):
    n, tall = mixed.shape[0] // 2, back_pieces[0].shape[0]
    steps = n // BLK
    half_rows = lambda width: pl.BlockSpec((BLK, width), lambda i, *_: (i + half * steps, 0))
    return call(
        functools.partial(out_kernel, tall - BLK),
        (steps,),
        [half_rows(2 * HD), half_rows(UNITS), fixed(2 * HD, D), *[fixed(tall, D)] * 4],
        rows_of(D),
        shape(n, D),
        flops=2 * n * D * (UNITS + 2 * HD),
        traffic=n * D * 2 + n * UNITS * 2 + D * UNITS * 2,
    )(base, mixed, active, dense_w, *back_pieces)


def pull_kernel(
    base, dq, dk, dv, du, tokens, mean, scale, gains, q0, q1, q2, q3, w, out, sums, wide, held
):
    @pl.when(pl.program_id(0) == 0)
    def _():
        sums[...] = jnp.zeros_like(sums)
        wide[...] = jnp.zeros_like(wide)

    add = lambda v: jnp.sum(v, axis=0, keepdims=True)
    for t, v in enumerate((dq, dk, dv)):
        wide[:, 2 * HD * t : 2 * HD * (t + 1)] += add(v[...].astype(F32))
    for r, q in enumerate((q0, q1, q2, q3)):
        for p in range(2):
            at = columns(place(base[0], r, p))
            one = (
                dot(dq[...], q[p, :, 0 : 2 * HD], 1, 1)
                + dot(dk[...], q[p, :, 2 * HD : 4 * HD], 1, 1)
                + dot(dv[...], q[p, :, 4 * HD :], 1, 1)
            )
            normal = (tokens[:, at].astype(F32) - mean[...]) * scale[...]
            sums[0:1, at] += add(one * normal)
            sums[1:2, at] += add(one)
            held[:, at] = one * gains[0:1, at]
    for r in range(4):
        for p in range(2):
            at = columns(place(base[1], r, p))
            two = dot(du[...], w[r, p], 1, 1)
            normal = (tokens[:, at].astype(F32) - mean[...]) * scale[...]
            sums[2:3, at] += add(two * normal)
            sums[3:4, at] += add(two)
            out[:, at] = (held[:, at] + two * gains[2:3, at]).astype(BF)


def pull_product(base, half, grads, du, tokens, mean, scale, gains, joined_pieces, pieces):
    n = du.shape[0] // 2
    steps = n // BLK
    half_rows = lambda width: pl.BlockSpec((BLK, width), lambda i, *_: (i + half * steps, 0))
    return call(
        pull_kernel,
        (steps,),
        [
            *[half_rows(2 * HD)] * 3,
            half_rows(UNITS),
            rows_of(D),
            half_rows(1),
            half_rows(1),
            fixed(4, D),
            *[fixed(2, BLK, WIDE)] * 4,
            fixed(4, 2, BLK, UNITS),
        ],
        [rows_of(D), fixed(4, D), fixed(1, WIDE)],
        [shape(n, D), shape(4, D, dtype=F32), shape(1, WIDE, dtype=F32)],
        [pltpu.VMEM((BLK, D), F32)],
        flops=2 * n * D * (UNITS + WIDE),
        traffic=n * D * 4 + n * UNITS * 4 + D * (UNITS + WIDE) * 2,
    )(base, *grads, du, tokens, mean, scale, gains, *joined_pieces, pieces)


def rows_grad_kernel(count, base, v, *refs):
    rights, outs = refs[:count], refs[count:]
    step = pl.program_id(0)
    v = v[...]
    parts, width = [], 0
    for right in rights:
        parts.append(dot(v, right[...], 0, 0).astype(BF))
    for j, out in enumerate(outs):

        @pl.when(step // 2 == j)
        def _(out=out):
            at = 0
            for part in parts:
                out[:, at : at + part.shape[1]] = part
                at += part.shape[1]


def rows_grad(base, v, rights, order):
    n, width = v.shape[0], sum(r.shape[1] for r in rights)

    def chosen(i, b):
        r = sum(jnp.where(i // 2 == j, r, 0) for j, r in enumerate(order))
        return (0, place(b[0], r, i % 2))

    def slot(j):
        return pl.BlockSpec((BLK, width), lambda i, b: (jnp.clip(i - 2 * j, 0, 1), 0))

    return call(
        functools.partial(rows_grad_kernel, len(rights)),
        (2 * len(order),),
        [pl.BlockSpec((n, BLK), chosen), *[fixed(*r.shape) for r in rights]],
        [slot(j) for j in range(len(order))],
        [shape(2 * BLK, width)] * len(order),
        flops=2 * n * BLK * 2 * len(order) * width,
        traffic=n * width * 2 + n * BLK * 4 * len(order),
    )(base, v, *rights)


def units_grad_kernel(v, near, far, out):
    n = near.shape[0]
    out[...] = (dot(v[:n], near[...], 0, 0) + dot(v[n:], far[...], 0, 0)).astype(BF)


def units_grad(v, near, far):
    n = v.shape[0]
    return call(
        units_grad_kernel,
        (UNITS // BLK,),
        [pl.BlockSpec((n, BLK), lambda i: (0, i)), fixed(n // 2, D), fixed(n // 2, D)],
        rows_of(D),
        shape(UNITS, D),
        flops=2 * n * UNITS * D,
        traffic=n * D * 2 + (n + D) * UNITS * 2,
        scalars=0,
    )(v, near, far)


def turn(v, cos, sin):
    lane = lax.broadcasted_iota(jnp.int32, v.shape, 1)
    half = ROT // 2
    swapped = jnp.where(lane < half, pltpu.roll(v, HD - half, 1), pltpu.roll(v, half, 1))
    return v * cos + swapped * sin


def attention_kernel(
    q, k, v, do, cq, sq, ck, sk, pq, eq, pk, ek, o, dq, dk, dv, ks, vs, dka, dva
):
    i = pl.program_id(2)
    scale = HD ** (-0.5)
    flat = lambda a: a.reshape(-1, HD)

    @pl.when(i == 0)
    def _():
        ks[...] = turn(flat(k[...]), ck[...], sk[...]).astype(BF)
        vs[...] = flat(v[...]).astype(BF)
        dka[...] = jnp.zeros_like(dka)
        dva[...] = jnp.zeros_like(dva)

    qr = turn(q[...], cq[...], sq[...]).astype(BF)
    s = dot(qr, ks[...], 1, 1) * scale
    allowed = (pk[...] <= pq[...]) & (ek[...] == eq[...])
    s = jnp.where(allowed, s, NEG)
    e = jnp.exp(s - jnp.max(s, axis=-1, keepdims=True))
    p = e / jnp.sum(e, axis=-1, keepdims=True)
    low = p.astype(BF)
    o[...] = dot(low, vs[...], 1, 0).astype(BF)
    dp = dot(do[...], vs[...], 1, 1)
    ds = (p * (dp - jnp.sum(p * dp, axis=-1, keepdims=True))).astype(BF)
    dq[...] = turn(dot(ds, ks[...], 1, 0) * scale, cq[...], -sq[...]).astype(BF)
    dva[...] += dot(low, do[...], 0, 0)
    dka[...] += dot(ds, qr, 0, 0)

    @pl.when(i == pl.num_programs(2) - 1)
    def _():
        dk[...] = turn(dka[...] * scale, ck[...], -sk[...]).astype(BF).reshape(dk.shape)
        dv[...] = dva[...].astype(BF).reshape(dv.shape)


def attention(joined, grad, cos, sin, pos, doc):
    half = 2 * BLK
    length = 2 * half
    joined = joined.reshape(2, 2, half, WIDE)
    grad = grad.reshape(2, 2, half, 2 * HD)
    part = lambda off: pl.BlockSpec(
        (None, None, BLK, HD), lambda s, h, i: (i // 2, s, i % 2, off + h)
    )
    whole = lambda off: pl.BlockSpec((2, None, half, HD), lambda s, h, i: (0, s, 0, off + h))
    tq = pl.BlockSpec((None, BLK, HD), lambda s, h, i: (s, i, 0))
    tk = pl.BlockSpec((None, length, HD), lambda s, h, i: (s, 0, 0))
    col = pl.BlockSpec((None, BLK, 1), lambda s, h, i: (s, i, 0))
    row = pl.BlockSpec((None, 1, length), lambda s, h, i: (s, 0, 0))
    results = call(
        attention_kernel,
        (2, 2, length // BLK),
        [part(0), whole(2), whole(4), part(0), tq, tq, tk, tk, col, col, row, row],
        [part(0), part(0), whole(0), whole(0)],
        [shape(2, 2, half, 2 * HD)] * 4,
        [
            pltpu.VMEM((length, HD), BF),
            pltpu.VMEM((length, HD), BF),
            pltpu.VMEM((length, HD), F32),
            pltpu.VMEM((length, HD), F32),
        ],
        flops=4 * length * length * HD * 14,
        traffic=4 * length * HD * 24,
        special=4 * length * length,
        scalars=0,
    )(
        joined, joined, joined, grad, cos, sin, cos, sin,
        pos[:, :, None], doc[:, :, None], pos[:, None, :], doc[:, None, :],
    )
    return [r.reshape(2 * length, 2 * HD) for r in results]


def column_plan(copies):
    units = FF // (16 * copies)
    for d in range(8):
        zl, x, core = d // 4, d // 2 % 2, d % 2
        for t in range(3):
            for m in range(2):
                head = core * 8 + zl * 4 + m * 2 + x
                yield 0, t * D + head * HD, HD, d, (t * 2 + m) * HD
        for zh in range(2):
            for y in range(copies):
                owner = (((zh * 2 + zl) * copies + y) * 2 + x) * 2 + core
                yield 1, owner * units, units, d, (zh * copies + y) * units


def deal_kernel(copies, wide, tall, wide_out, tall_out):
    pairs = ((wide, wide_out), (tall, tall_out))
    for which, start, width, d, at in column_plan(copies):
        source, target = pairs[which]
        target[d, :, at : at + width] = source[:, start : start + width]


def deal_columns(wide, tall, copies):
    rows = wide.shape[0]
    return call(
        functools.partial(deal_kernel, copies),
        (1,),
        [fixed(*wide.shape), fixed(*tall.shape)],
        [fixed(8, rows, WIDE), fixed(8, rows, UNITS)],
        [shape(8, rows, WIDE), shape(8, rows, UNITS)],
        traffic=rows * (3 * D + FF) * 4,
        scalars=0,
    )(wide, tall)


def collect_kernel(copies, which_one, source, target):
    for which, start, width, d, at in column_plan(copies):
        if which == which_one:
            target[:, start : start + width] = source[d, :, at : at + width].astype(F32)


def collect_columns(v, which, copies):
    rows, width = v.shape[1], (3 * D, FF)[which]
    return call(
        functools.partial(collect_kernel, copies, which),
        (1,),
        [fixed(*v.shape)],
        fixed(rows, width),
        shape(rows, width, dtype=F32),
        traffic=rows * width * 6,
        scalars=0,
    )(v)


def pack_kernel(*refs):
    for j, v in enumerate(refs[:-1]):
        refs[-1][j : j + 1, 0 : v.shape[1]] = v[...]


def pack_rows(vectors):
    vectors = [v[None] for v in vectors]
    return call(
        pack_kernel,
        (1,),
        [fixed(*v.shape) for v in vectors],
        fixed(len(vectors), BLK),
        shape(len(vectors), BLK),
        scalars=0,
    )(*vectors)


def swap(v, axes=("zl", "x", "core")):
    return lax.all_to_all(v, axes, 0, 0, tiled=True)


def gather_plain(v, split):
    return split(lax.all_gather(v, ("zh", "y"), axis=0, tiled=False))


def half_sum(v, other):
    return (v.astype(F32) + other.astype(F32)).astype(BF)


def split_rows(copies):
    def split(w):
        c = w.shape[-1]
        w = w.reshape(2, copies, 2, -1, c).transpose(0, 2, 1, 3, 4).reshape(2, 2, 2, BLK, c)
        return [w[a, :, b] for a in (0, 1) for b in (0, 1)]

    return split


def join_rows(copies):
    def join(w):
        c = w.shape[-1]
        w = w.reshape(2, 2, 2, BLK, c).transpose(0, 2, 1, 3, 4)
        w = w.reshape(2, 2, copies, -1, c).transpose(0, 2, 1, 3, 4)
        return w.reshape(2 * copies, -1, c)

    return join


def dense_parts(pieces):
    zh, y, core = (lax.axis_index(a) for a in ("zh", "y", "core"))
    w = jnp.stack(pieces).reshape(2, 2, HD // 2, D)
    w = jnp.where(y == 0, w, w[:, ::-1])
    same = zh == core
    return jnp.where(same, w[0], w[1]), jnp.where(same, w[1], w[0])


def dense_join(keep, other):
    first = lax.axis_index("core") == 0
    low, high = jnp.where(first, keep, other), jnp.where(first, other, keep)
    return jnp.stack([low, high], axis=1).reshape(2 * HD, D)


def dense_split(g):
    first = lax.axis_index("core") == 0
    g = g.reshape(2, 2, HD // 2, D)
    return jnp.where(first, g[:, 0], g[:, 1]), jnp.where(first, g[:, 1], g[:, 0])


def dense_sort(keep, other):
    same = lax.axis_index("zh") == lax.axis_index("core")
    w = jnp.stack([jnp.where(same, keep, other), jnp.where(same, other, keep)])
    return jnp.where(lax.axis_index("y") == 0, w, w[:, ::-1])


def gather_dense_plain(w):
    core, x = lax.axis_index("core"), lax.axis_index("x")
    w = lax.all_gather(w, ("zh", "y", "x", "core"), axis=0, tiled=True).reshape(2, 2, 2, HD, D)
    w = lax.dynamic_slice(w, (core, 0, x, 0, 0), (1, 2, 1, HD, D))
    return w.reshape(2 * HD, D)


def reduce_dense_plain(g):
    core, x = lax.axis_index("core"), lax.axis_index("x")
    w = jnp.zeros((2, 2, 2, HD, D), F32)
    g = g.astype(F32).reshape(1, 2, 1, HD, D)
    w = lax.dynamic_update_slice(w, g, (core, 0, x, 0, 0)).reshape(-1, D)
    return lax.psum_scatter(w, ("zh", "y", "x", "core"), scatter_dimension=0, tiled=True)


def shards(
    copies,
    block_input,
    output_grad,
    documents,
    span_order,
    attention_norm_gain,
    attention_norm_bias,
    query_key_value_weight,
    query_key_value_bias,
    dense_weight,
    dense_bias,
    mlp_norm_gain,
    mlp_norm_bias,
    to_hidden_weight,
    to_hidden_bias,
    from_hidden_weight,
    from_hidden_bias,
):
    span = block_input.shape[1]
    count = 16 * copies
    rows = D // count
    units = FF // count
    length = 4 * span
    zl, x, core = (lax.axis_index(a) for a in ("zl", "x", "core"))
    own_in, own_grad = block_input[0], output_grad[0]
    base = jnp.zeros((2,), jnp.int32)
    if copies == 2:
        base = base.at[0].set(lax.axis_index("zh") * 2 + lax.axis_index("y"))

    def spread_small(first):
        vectors = (
            first,
            attention_norm_bias,
            mlp_norm_gain,
            mlp_norm_bias,
            dense_bias,
            from_hidden_bias,
            query_key_value_bias,
            to_hidden_bias,
        )
        if copies == 2:
            small = pack_rows(vectors)
        else:
            small = jnp.stack([jnp.pad(v, (0, BLK - v.shape[0])) for v in vectors])
        facts = jnp.concatenate([documents[0], jnp.pad(span_order[0], (0, length - 4))])
        small = jnp.concatenate([small, facts.astype(BF).reshape(8, BLK)], axis=0)
        small = jnp.broadcast_to(small[None], (count, 16, BLK)).reshape(count * 16, BLK)
        return swap(small, AXES)

    def unpack(small):
        small = small.reshape(count, 16, BLK)
        row = (lax.axis_index("zh") * 2 * copies + lax.axis_index("y")) * 4
        facts = [lax.dynamic_slice(small, (row + s * copies * 4, 8, 0), (1, 8, BLK)) for s in (zl, 1 - zl)]
        facts = [v.astype(jnp.int32).reshape(2 * length) for v in facts]
        small = small[:, :8].astype(F32)
        take = lambda j, n: small[:, j, :n].reshape(-1)
        gains = jnp.stack([take(j, rows) for j in range(4)])
        out_shift = take(4, rows) + take(5, rows)
        joined_shift = take(6, 3 * rows).reshape(3, 2, 2, 2, 2, HD)
        joined_shift = lax.dynamic_slice(joined_shift, (0, core, zl, 0, x, 0), (3, 1, 1, 2, 1, HD))
        joined_shift = joined_shift.reshape(1, WIDE)
        hidden_shift = take(7, units).reshape(2, 2, copies, 2, 2, units)
        hidden_shift = lax.dynamic_slice(
            hidden_shift, (0, zl, 0, x, core, 0), (2, 1, copies, 1, 1, units)
        ).reshape(1, UNITS)

        offsets = jnp.arange(span, dtype=jnp.int32)
        pos, doc = [], []
        for known in facts:
            for c in (0, 1):
                for b in (0, 1):
                    block = (x ^ b) * 2 + (core ^ c)
                    doc.append(lax.dynamic_slice(known, (block * span,), (span,)))
                    pos.append(lax.dynamic_slice(known, (length + block,), (1,)) * span + offsets)
        pos = jnp.concatenate(pos).reshape(2, length)
        doc = jnp.concatenate(doc).reshape(2, length)
        inverse = jnp.power(THETA, -jnp.arange(ROT // 2, dtype=F32) * (2.0 / ROT))
        angles = pos.astype(F32)[:, :, None] * inverse
        cosine, sine = jnp.cos(angles), jnp.sin(angles)
        rest = jnp.zeros((2, length, HD - ROT), F32)
        cos_table = jnp.concatenate([cosine, cosine, rest + 1.0], axis=-1)
        sin_table = jnp.concatenate([-sine, sine, rest], axis=-1)


        return gains, out_shift, joined_shift, hidden_shift, pos, doc, cos_table, sin_table

    order = (3, 1, 2, 0)
    ordered = lambda v: [v[order.index(r)] for r in range(4)]
    halves = lambda v: (v[: v.shape[0] // 2], v[v.shape[0] // 2 :])
    join = lambda *v: jnp.concatenate(v, axis=0)
    block = lambda v, f: v[f * span : (f + 1) * span]
    low_sum = lambda v, w: (v.astype(F32) + w.astype(F32)).astype(BF)
    pair = copies == 2

    def near(d, own, names):
        return join(own, *[d[n] for n in names.split()])

    tasks, parts = {}, {}

    def once(name, make):
        if name not in parts:
            parts[name] = make()
        return parts[name]

    facts_of = lambda d: once("facts", lambda: unpack(d["ss"]))

    def move(name, axis, source):
        tasks[name] = (source, lambda v, d: flip(v, axis))

    def kernel(name, source, step):
        tasks[name] = (source, step)

    kernel(
        "deal",
        lambda d: query_key_value_weight,
        lambda v, d: deal_columns(v, to_hidden_weight, copies),
    )
    tasks["sw"] = (lambda d: d["deal"][0], lambda v, d: swap(v).reshape(2, 4 * rows, WIDE))
    tasks["st"] = (lambda d: d["deal"][1], lambda v, d: swap(v).reshape(2, 4 * rows, UNITS))
    tasks["ss"] = (lambda d: attention_norm_gain, lambda v, d: spread_small(v))
    chunk = jnp.concatenate([dense_weight, from_hidden_weight], axis=0)
    move("An", "y", lambda d: chunk)
    move("A0z", "zh", lambda d: halves(chunk)[0])
    move("A1z", "zh", lambda d: halves(chunk)[1])
    move("Af0", "y", lambda d: d["A0z"])
    move("Af1", "y", lambda d: d["A1z"])
    move("Wn", "y", lambda d: d["sw"])
    move("Wz", "zh", lambda d: d["sw"])
    move("Wf", "y", lambda d: d["Wz"])
    late = lambda v, d: after(v, d["A"][0])
    back_of = lambda d: [
        chunk,
        d["An"],
        join(late(d["A0z"], d), late(d["A1z"], d)),
        join(late(d["Af0"], d), late(d["Af1"], d)),
    ]
    back = lambda d: once("back", lambda: back_of(d))
    wide = lambda d: [d["sw"], d["Wn"], d["Wz"], d["Wf"]]
    tasks["Tg"] = (
        lambda d: d["st"],
        lambda v, d: lax.all_gather(v, ("zh", "y"), axis=0, tiled=False),
    )
    tasks["Br"] = (
        lambda d: d["B"],
        lambda v, d: lax.psum_scatter(v, ("zh", "y"), scatter_dimension=0, tiled=True),
    )
    tall_of = lambda d: d["Tg"] if pair else jnp.stack(split_rows(copies)(d["Tg"]))
    tall = lambda d: once("tall", lambda: tall_of(d))
    if not pair:
        back_of = lambda d: gather_plain(from_hidden_weight, lambda w: list(w.reshape(4, BLK, D)))
        wide = lambda d: once("wide", lambda: gather_plain(d["sw"], split_rows(copies)))
    dense_two_of = lambda d: dense_parts([p[:rows] for p in (chunk, d["An"], d["A0z"], d["Af0"])])
    dense_two = lambda d: once("dense_two", lambda: dense_two_of(d))
    move("dc", "core", lambda d: dense_two(d)[1])
    dense_of = lambda d: dense_join(dense_two(d)[0], d["dc"])
    dense = lambda d: once("dense", lambda: dense_of(d))
    if not pair:
        dense_of = lambda d: gather_dense_plain(dense_weight)

    for n, own in (("i", own_in), ("u", own_grad)):
        move(n + "x", "x", lambda d, own=own: own)
        move(n + "z", "zl", lambda d, own=own: own)
        move(n + "b", "x", lambda d, n=n: d[n + "z"])
        move(n + "0", "core", lambda d, own=own: own)
        move(n + "1", "core", lambda d, n=n: d[n + "x"])
        move(n + "2", "core", lambda d, n=n: d[n + "z"])
        move(n + "3", "core", lambda d, n=n: d[n + "b"])
    tokens_of = lambda d: (near(d, own_in, "ix iz ib"), join(*[d[n] for n in ("i0", "i1", "i2", "i3")]))
    tokens = lambda d: once("tokens", lambda: tokens_of(d))
    upstream_of = lambda d: (near(d, own_grad, "ux uz ub"), join(*[d[n] for n in ("u0", "u1", "u2", "u3")]))
    upstream = lambda d: once("upstream", lambda: upstream_of(d))

    kernel("norms", lambda d: facts_of(d)[0], lambda v, d: norms(*tokens(d), v))
    kernel("dO", lambda d: dense(d), lambda v, d: mixed_grad(*upstream(d), v))
    kernel(
        "joined",
        lambda d: d["norms"][0],
        lambda v, d: joined_product(base, v, wide(d), facts_of(d)[2]),
    )
    kernel(
        "A",
        lambda d: (d["joined"], d["dO"])[0],
        lambda v, d: attention(v, d["dO"], *[facts_of(d)[j] for j in (6, 7, 4, 5)]),
    )
    heads = lambda d: d["A"]
    kernel(
        "W",
        lambda d: d["norms"][0],
        lambda v, d: ordered(rows_grad(base, v, heads(d)[1:], order)),
    )
    kernel(
        "H",
        lambda d: d["norms"][1],
        lambda v, d: hidden_products(base, v, *upstream(d), tall(d), back(d), facts_of(d)[3]),
    )
    kernel(
        "T",
        lambda d: d["H"][1],
        lambda v, d: ordered(rows_grad(base, d["norms"][1], [v], order)),
    )
    kernel(
        "B", lambda d: d["H"][0], lambda v, d: units_grad(v, *upstream(d))
    )
    for h, n in ((1, "f"), (0, "n")):
        kernel(
            "P" + n,
            lambda d: d["H"][1],
            lambda v, d, h=h: pull_product(
                base, h, heads(d)[1:], v, tokens(d)[h], *d["norms"][2:], facts_of(d)[0], wide(d), tall(d)
            ),
        )
        kernel(
            "O" + n,
            lambda d: d["H"][0],
            lambda v, d, h=h: out_product(base, h, heads(d)[0], v, dense(d), back(d)),
        )

    def grad_dense(d):
        mixed, (near_up, far_up) = heads(d)[0], upstream(d)
        low, high = halves(mixed)
        return (dot(low, near_up, 0, 0) + dot(high, far_up, 0, 0)).astype(BF)

    g_dense = lambda d: once("g_dense", lambda: grad_dense(d))
    g_sort = lambda d: once("sort", lambda: dense_sort(dense_split(g_dense(d))[0], d["gd"]))
    for n in "WT":
        move(n + "3", "y", lambda d, n=n: d[n][3])
        move(n + "1", "y", lambda d, n=n: d[n][1])
    far_sum = lambda d, n: once(n + "far", lambda: low_sum(d[n][2], d[n + "3"]))
    move("zW", "zh", lambda d: far_sum(d, "W"))
    move("zT0", "zh", lambda d: halves(far_sum(d, "T"))[0])
    move("zT1", "zh", lambda d: halves(far_sum(d, "T"))[1])
    move("gd", "core", lambda d: dense_split(g_dense(d))[1])
    move("D1", "y", lambda d: g_sort(d)[:, 1])
    dense_y = lambda d: once("dense_y", lambda: g_sort(d)[:, 0].astype(F32) + d["D1"].astype(F32))
    move("zD", "zh", lambda d: dense_y(d)[1].astype(BF))
    add = lambda d, n, far: d[n][0].astype(F32) + d[n + "1"].astype(F32) + far.astype(F32)

    for n, k in (("p", "P"), ("o", "O")):
        part = lambda d, which, k=k: d[k + which][0] if k == "P" else d[k + which]
        total = lambda d, f, n=n, part=part: block(part(d, "n"), f).astype(F32) + d[f"{n}c{f}"].astype(F32)
        for f in range(4):
            move(f"{n}c{f}", "core", lambda d, f=f, part=part: block(part(d, "f"), f))
        move(n + "3", "x", lambda d, total=total: total(d, 3).astype(BF))
        move(n + "1", "x", lambda d, total=total: total(d, 1).astype(BF))
        move(
            n + "z",
            "zl",
            lambda d, n=n, total=total: (total(d, 2) + d[n + "3"].astype(F32)).astype(BF),
        )
        tasks[n] = lambda d, n=n, total=total: (
            total(d, 0) + d[n + "1"].astype(F32) + d[n + "z"].astype(F32)
        )

    grad_own = own_grad.astype(F32)

    def all_sums(v, w, hidden_sum):
        joined_sum = lax.dynamic_update_slice(
            jnp.zeros((3, 2, 2, 2, 2, HD), F32),
            (v[2] + w[2]).reshape(3, 1, 1, 2, 1, HD),
            (0, core, zl, 0, x, 0),
        )
        hidden_sum = lax.dynamic_update_slice(
            jnp.zeros((2, 2, copies, 2, 2, units), F32),
            hidden_sum.reshape(2, 1, copies, 1, 1, units),
            (0, zl, 0, x, core, 0),
        )
        sums = [*(v[1] + w[1]), jnp.sum(grad_own, axis=0), joined_sum, hidden_sum]
        return jnp.concatenate([s.reshape(count, -1) for s in sums], axis=1)

    tasks["gs"] = (
        lambda d: all_sums(d["Pn"], d["Pf"], d["H"][2]),
        lambda v, d: jnp.sum(swap(v, AXES), axis=0),
    )
    tasks["gw"] = (
        lambda d: add(d, "W", d["zW"]).astype(BF).reshape(8, rows, WIDE),
        lambda v, d: swap(v),
    )
    tasks["gt"] = (
        lambda d: add(d, "T", join(d["zT0"], d["zT1"])).astype(BF).reshape(8, rows, UNITS),
        lambda v, d: swap(v),
    )

    if pair:
        d = run(tasks)
        pull, out = tasks["p"](d), tasks["o"](d)
        sums, grad_wide, grad_tall = d["gs"], d["gw"], d["gt"]
        grad_dense = dense_y(d)[0] + d["zD"].astype(F32)
    else:
        names = [*CFG["y"], *CFG["zh"], "dc", "gd", "gw", "gt"]
        d = run(tasks, names)
        pull, out, sums = tasks["p"](d), tasks["o"](d), d["gs"]

        def scatter(pieces, plan):
            w = plan(jnp.stack(pieces).astype(F32))
            return lax.psum_scatter(w, ("zh", "y"), scatter_dimension=0, tiled=False)

        grad_wide = swap(scatter(d["W"], join_rows(copies)).astype(BF).reshape(8, rows, WIDE))
        grad_tall = swap(scatter(d["T"], join_rows(copies)).astype(BF).reshape(8, rows, UNITS))
        grad_dense = reduce_dense_plain(g_dense(d))

    grad_back = d["Br"].astype(F32)
    out_shift = facts_of(d)[1]
    grad_wide = collect_columns(grad_wide, 0, copies)
    grad_tall = collect_columns(grad_tall, 1, copies)

    own_wide = own_in.astype(F32)
    block_output = (own_wide + (out + out_shift)).astype(BF)[None]
    own_centre = own_wide - jnp.mean(own_wide, axis=-1, keepdims=True)
    own_spread = lax.rsqrt(jnp.mean(own_centre * own_centre, axis=-1, keepdims=True) + EPS)
    own_normal = own_centre * own_spread
    pull = own_spread * (
        pull
        - jnp.mean(pull, axis=-1, keepdims=True)
        - own_normal * jnp.mean(pull * own_normal, axis=-1, keepdims=True)
    )
    input_grad = (grad_own + pull).astype(BF)[None]

    cut = lambda a, n: sums[a : a + n]
    bias_sum = cut(4 * rows, rows)


    return (
        block_output,
        input_grad,
        cut(0, rows),
        cut(rows, rows),
        grad_wide,
        cut(5 * rows, 3 * rows),
        grad_dense,
        bias_sum,
        cut(2 * rows, rows),
        cut(3 * rows, rows),
        grad_tall,
        cut(8 * rows, units),
        grad_back,
        bias_sum,
    )


def solution(mesh):
    copies = mesh.shape["batch"] // 4
    inner = Mesh(mesh.devices.reshape(2, 2, copies, 2, 2), AXES)
    batch, ctx = AXES[:3], AXES[3:]
    tokens = P(batch, ctx, None)
    vector, matrix = P(AXES), P(AXES, None)
    params = (vector, vector, matrix, vector, matrix, vector)
    return jax.shard_map(
        functools.partial(shards, copies),
        mesh=inner,
        in_specs=(tokens, tokens, P(batch, None), P(batch, None)) + params + params,
        out_specs=(tokens, tokens) + params + params,
        check_vma=False,
    )
```

```python
import functools

import jax
import jax.numpy as jnp
from jax import lax
from jax.experimental import pallas as pl
from jax.experimental.pallas import tpu as pltpu
from jax.sharding import Mesh, PartitionSpec as P

D = 2048
H = 16
HD = 128
ROT = 32
FF = 8192
WIDE = 6 * HD
UNITS = FF // 8
BLK = 256
NBLK = D // BLK
EPS = 1e-05
NEG = -1e30
THETA = 10000.0
BF = jnp.bfloat16
F32 = jnp.float32
AXES = ("zh", "zl", "y", "x", "core")
VMEM = 50 * 2**20
COST = 1.0


CFG = {
    "swap": ["sw", "st", "ss", "gs", "gw", "gt"],
    "kernel": ["deal", "norms", "joined", "dO", "A", "W", "H", "T", "B", "Pf", "Pn", "Of", "On"],
    "x": ["ix", "ib", "ux", "ub", "p3", "p1", "o3", "o1"],
    "zl": ["iz", "uz", "pz", "oz"],
    "core": ["i0", "i1", "i2", "i3", "u0", "u1", "u2", "u3", "dc", "gd", "pc3", "pc1", "pc2", "pc0", "oc3", "oc1", "oc2", "oc0"],
    "y": ["An", "Wn", "Af0", "Wf", "Af1", "W3", "T3", "D1", "W1", "T1"],
    "zh": ["A0z", "Wz", "A1z", "zW", "zT0", "zD", "zT1"],
    "sc": ["Tg", "Br"],
    "depth": {"core": 3},
    "ties": {
        "T": ["W3"],
        "Pf": ["zW", "T3"],
        "Of": ["zT0"],
        "o3": ["W1", "gs"],
        "o1": ["zT1", "T1"],
        "oz": ["gw"],
    },
}


def after(v, *others):
    return lax.optimization_barrier((v, *others))[0]


def flip(v, axis):
    return lax.ppermute(v, axis, [(0, 1), (1, 0)])


def run(tasks, skip=()):
    channels = ("swap", "kernel", "x", "zl", "core", "y", "zh", "sc")
    lines = {c: [n for n in CFG[c] if n not in skip] for c in channels}
    done, at = {}, dict.fromkeys(lines, 0)
    first = lambda v: v[0] if isinstance(v, (list, tuple)) else v
    while any(at[c] < len(lines[c]) for c in lines):
        moved = False
        for c, names in lines.items():
            while at[c] < len(names):
                name = names[at[c]]
                source, step = tasks[name]
                waits = [w for w in CFG["ties"].get(name, ()) if w not in skip]
                place = at[c] - CFG["depth"].get(c, 1)
                if place >= 0:
                    waits.append(names[place])
                if any(w not in done for w in waits):
                    break
                try:
                    v = source(done)
                    if waits:
                        v = after(v, *[first(done[w]) for w in waits])
                    done[name] = step(v, done)
                except KeyError:
                    break
                at[c] += 1
                moved = True
        assert moved
    return done


def dot(a, b, ca, cb):
    return lax.dot_general(a, b, (((ca,), (cb,)), ((), ())), preferred_element_type=F32)


def call(kernel, grid, ins, outs, shapes, scratch=(), flops=0, traffic=0, special=0, scalars=1):
    return pl.pallas_call(
        kernel,
        grid_spec=pltpu.PrefetchScalarGridSpec(
            num_scalar_prefetch=scalars,
            grid=grid,
            in_specs=ins,
            out_specs=outs,
            scratch_shapes=scratch,
        ),
        out_shape=shapes,
        compiler_params=pltpu.CompilerParams(vmem_limit_bytes=VMEM),
        cost_estimate=pl.CostEstimate(
            flops=int(flops * COST), bytes_accessed=int(traffic * COST), transcendentals=int(special * COST)
        ),
    )


def shape(*dims, dtype=BF):
    return jax.ShapeDtypeStruct(dims, dtype)


def fixed(*dims):
    return pl.BlockSpec(dims, lambda *_: (0,) * len(dims))


def rows_of(width, rows=BLK):
    return pl.BlockSpec((rows, width), lambda i, *_: (i, 0))


def two_halves(width):
    return [
        pl.BlockSpec((BLK, width), lambda i, *_: (jnp.minimum(i, 3), 0)),
        pl.BlockSpec((BLK, width), lambda i, *_: (jnp.maximum(i - 4, 0), 0)),
    ]


def pick(near, far):
    return jnp.where(pl.program_id(0) < 4, near[...], far[...])


def place(base, r, p):
    s = r ^ base
    return (s // 2) * 4 + p * 2 + s % 2


def columns(index):
    return pl.ds(pl.multiple_of(index * BLK, BLK), BLK)


def norm_kernel(near, far, gains, one, two, mean, scale):
    v = pick(near, far).astype(F32)
    mu = jnp.mean(v, axis=-1, keepdims=True)
    v = v - mu
    r = lax.rsqrt(jnp.mean(v * v, axis=-1, keepdims=True) + EPS)
    v = v * r
    one[...] = (v * gains[0:1] + gains[1:2]).astype(BF)
    two[...] = (v * gains[2:3] + gains[3:4]).astype(BF)
    mean[...] = mu
    scale[...] = r


def norms(near, far, gains):
    n = 2 * near.shape[0]
    return call(
        norm_kernel,
        (n // BLK,),
        [*two_halves(D), fixed(4, D)],
        [rows_of(D), rows_of(D), rows_of(1), rows_of(1)],
        [shape(n, D), shape(n, D), shape(n, 1, dtype=F32), shape(n, 1, dtype=F32)],
        traffic=n * D * 6,
        flops=n * D * 10,
        scalars=0,
    )(near, far, gains)


def joined_kernel(base, v, w0, w1, w2, w3, shift, out):
    total = jnp.zeros((BLK, WIDE), F32) + shift[...]
    for r, w in enumerate((w0, w1, w2, w3)):
        for p in range(2):
            total += dot(v[:, columns(place(base[0], r, p))], w[p], 1, 0)
    out[...] = total


def joined_product(base, v, pieces, shift):
    n = v.shape[0]
    return call(
        joined_kernel,
        (n // BLK,),
        [rows_of(D), *[fixed(2, BLK, WIDE)] * 4, fixed(1, WIDE)],
        rows_of(WIDE),
        shape(n, WIDE, dtype=F32),
        flops=2 * n * D * WIDE,
        traffic=n * D * 2 + n * WIDE * 4 + D * WIDE * 2,
    )(base, v, *pieces, shift)


def mixed_grad_kernel(near, far, w, out):
    out[...] = dot(pick(near, far), w[...], 1, 1).astype(BF)


def mixed_grad(near, far, w):
    n, wide = 2 * near.shape[0], w.shape[0]
    return call(
        mixed_grad_kernel,
        (n // BLK,),
        [*two_halves(D), fixed(wide, D)],
        rows_of(wide),
        shape(n, wide),
        flops=2 * n * D * wide,
        traffic=n * D * 2,
        scalars=0,
    )(near, far, w)


def hidden_kernel(
    skip, base, v, near, far, w, b0, b1, b2, b3, shift, active, grad, sums, back
):
    up = pick(near, far)
    for r, b in enumerate((b0, b1, b2, b3)):
        back[:, columns(r ^ base[0])] = dot(up, b[skip:], 1, 1)
    u = jnp.zeros((BLK, UNITS), F32) + shift[...]
    for r in range(4):
        for p in range(2):
            u += dot(v[:, columns(place(base[1], r, p))], w[r, p], 1, 0)
    below = 0.5 * (1.0 + lax.erf(u * (0.5**0.5)))
    active[...] = (u * below).astype(BF)
    slope = below + u * jnp.exp(-0.5 * u * u) * ((2.0 * jnp.pi) ** (-0.5))
    low = (back[...] * slope).astype(BF)
    grad[...] = low

    @pl.when(pl.program_id(0) == 0)
    def _():
        sums[...] = jnp.zeros_like(sums)

    sums[...] += jnp.sum(low.astype(F32), axis=0, keepdims=True)


def hidden_products(base, v, near, far, pieces, back_pieces, shift):
    n, tall = v.shape[0], back_pieces[0].shape[0]
    return call(
        functools.partial(hidden_kernel, tall - BLK),
        (n // BLK,),
        [rows_of(D), *two_halves(D), fixed(4, 2, BLK, UNITS), *[fixed(tall, D)] * 4, fixed(1, UNITS)],
        [rows_of(UNITS), rows_of(UNITS), fixed(1, UNITS)],
        [shape(n, UNITS), shape(n, UNITS), shape(1, UNITS, dtype=F32)],
        [pltpu.VMEM((BLK, UNITS), F32)],
        flops=4 * n * D * UNITS,
        traffic=n * D * 4 + n * UNITS * 4 + D * UNITS * 4,
        special=2 * n * UNITS,
    )(base, v, near, far, pieces, *back_pieces, shift)


def out_kernel(skip, base, mixed, active, w, b0, b1, b2, b3, out):
    total = dot(mixed[...], w[...], 1, 0)
    for r, b in enumerate((b0, b1, b2, b3)):
        total += dot(active[:, columns(r ^ base[0])], b[skip:], 1, 0)
    out[...] = total.astype(BF)


def out_product(base, half, mixed, active, dense_w, back_pieces):
    n, tall = mixed.shape[0] // 2, back_pieces[0].shape[0]
    steps = n // BLK
    half_rows = lambda width: pl.BlockSpec((BLK, width), lambda i, *_: (i + half * steps, 0))
    return call(
        functools.partial(out_kernel, tall - BLK),
        (steps,),
        [half_rows(2 * HD), half_rows(UNITS), fixed(2 * HD, D), *[fixed(tall, D)] * 4],
        rows_of(D),
        shape(n, D),
        flops=2 * n * D * (UNITS + 2 * HD),
        traffic=n * D * 2 + n * UNITS * 2 + D * UNITS * 2,
    )(base, mixed, active, dense_w, *back_pieces)


def pull_kernel(
    base, dq, dk, dv, du, tokens, mean, scale, gains, q0, q1, q2, q3, w, out, sums, wide, held
):
    @pl.when(pl.program_id(0) == 0)
    def _():
        sums[...] = jnp.zeros_like(sums)
        wide[...] = jnp.zeros_like(wide)

    add = lambda v: jnp.sum(v, axis=0, keepdims=True)
    for t, v in enumerate((dq, dk, dv)):
        wide[:, 2 * HD * t : 2 * HD * (t + 1)] += add(v[...].astype(F32))
    for r, q in enumerate((q0, q1, q2, q3)):
        for p in range(2):
            at = columns(place(base[0], r, p))
            one = (
                dot(dq[...], q[p, :, 0 : 2 * HD], 1, 1)
                + dot(dk[...], q[p, :, 2 * HD : 4 * HD], 1, 1)
                + dot(dv[...], q[p, :, 4 * HD :], 1, 1)
            )
            normal = (tokens[:, at].astype(F32) - mean[...]) * scale[...]
            sums[0:1, at] += add(one * normal)
            sums[1:2, at] += add(one)
            held[:, at] = one * gains[0:1, at]
    for r in range(4):
        for p in range(2):
            at = columns(place(base[1], r, p))
            two = dot(du[...], w[r, p], 1, 1)
            normal = (tokens[:, at].astype(F32) - mean[...]) * scale[...]
            sums[2:3, at] += add(two * normal)
            sums[3:4, at] += add(two)
            out[:, at] = (held[:, at] + two * gains[2:3, at]).astype(BF)


def pull_product(base, half, grads, du, tokens, mean, scale, gains, joined_pieces, pieces):
    n = du.shape[0] // 2
    steps = n // BLK
    half_rows = lambda width: pl.BlockSpec((BLK, width), lambda i, *_: (i + half * steps, 0))
    return call(
        pull_kernel,
        (steps,),
        [
            *[half_rows(2 * HD)] * 3,
            half_rows(UNITS),
            rows_of(D),
            half_rows(1),
            half_rows(1),
            fixed(4, D),
            *[fixed(2, BLK, WIDE)] * 4,
            fixed(4, 2, BLK, UNITS),
        ],
        [rows_of(D), fixed(4, D), fixed(1, WIDE)],
        [shape(n, D), shape(4, D, dtype=F32), shape(1, WIDE, dtype=F32)],
        [pltpu.VMEM((BLK, D), F32)],
        flops=2 * n * D * (UNITS + WIDE),
        traffic=n * D * 4 + n * UNITS * 4 + D * (UNITS + WIDE) * 2,
    )(base, *grads, du, tokens, mean, scale, gains, *joined_pieces, pieces)


def rows_grad_kernel(count, base, v, *refs):
    rights, outs = refs[:count], refs[count:]
    step = pl.program_id(0)
    v = v[...]
    parts, width = [], 0
    for right in rights:
        parts.append(dot(v, right[...], 0, 0).astype(BF))
    for j, out in enumerate(outs):

        @pl.when(step // 2 == j)
        def _(out=out):
            at = 0
            for part in parts:
                out[:, at : at + part.shape[1]] = part
                at += part.shape[1]


def rows_grad(base, v, rights, order):
    n, width = v.shape[0], sum(r.shape[1] for r in rights)

    def chosen(i, b):
        r = sum(jnp.where(i // 2 == j, r, 0) for j, r in enumerate(order))
        return (0, place(b[0], r, i % 2))

    def slot(j):
        return pl.BlockSpec((BLK, width), lambda i, b: (jnp.clip(i - 2 * j, 0, 1), 0))

    return call(
        functools.partial(rows_grad_kernel, len(rights)),
        (2 * len(order),),
        [pl.BlockSpec((n, BLK), chosen), *[fixed(*r.shape) for r in rights]],
        [slot(j) for j in range(len(order))],
        [shape(2 * BLK, width)] * len(order),
        flops=2 * n * BLK * 2 * len(order) * width,
        traffic=n * width * 2 + n * BLK * 4 * len(order),
    )(base, v, *rights)


def units_grad_kernel(v, near, far, out):
    n = near.shape[0]
    out[...] = (dot(v[:n], near[...], 0, 0) + dot(v[n:], far[...], 0, 0)).astype(BF)


def units_grad(v, near, far):
    n = v.shape[0]
    return call(
        units_grad_kernel,
        (UNITS // BLK,),
        [pl.BlockSpec((n, BLK), lambda i: (0, i)), fixed(n // 2, D), fixed(n // 2, D)],
        rows_of(D),
        shape(UNITS, D),
        flops=2 * n * UNITS * D,
        traffic=n * D * 2 + (n + D) * UNITS * 2,
        scalars=0,
    )(v, near, far)


def turn(v, cos, sin):
    lane = lax.broadcasted_iota(jnp.int32, v.shape, 1)
    half = ROT // 2
    swapped = jnp.where(lane < half, pltpu.roll(v, HD - half, 1), pltpu.roll(v, half, 1))
    return v * cos + swapped * sin


def attention_kernel(
    q, k, v, do, cq, sq, ck, sk, pq, eq, pk, ek, o, dq, dk, dv, ks, vs, dka, dva
):
    i = pl.program_id(2)
    scale = HD ** (-0.5)
    flat = lambda a: a.reshape(-1, HD)

    @pl.when(i == 0)
    def _():
        ks[...] = turn(flat(k[...]), ck[...], sk[...]).astype(BF)
        vs[...] = flat(v[...]).astype(BF)
        dka[...] = jnp.zeros_like(dka)
        dva[...] = jnp.zeros_like(dva)

    qr = turn(q[...], cq[...], sq[...]).astype(BF)
    s = dot(qr, ks[...], 1, 1) * scale
    allowed = (pk[...] <= pq[...]) & (ek[...] == eq[...])
    s = jnp.where(allowed, s, NEG)
    e = jnp.exp(s - jnp.max(s, axis=-1, keepdims=True))
    p = e / jnp.sum(e, axis=-1, keepdims=True)
    low = p.astype(BF)
    o[...] = dot(low, vs[...], 1, 0).astype(BF)
    dp = dot(do[...], vs[...], 1, 1)
    ds = (p * (dp - jnp.sum(p * dp, axis=-1, keepdims=True))).astype(BF)
    dq[...] = turn(dot(ds, ks[...], 1, 0) * scale, cq[...], -sq[...]).astype(BF)
    dva[...] += dot(low, do[...], 0, 0)
    dka[...] += dot(ds, qr, 0, 0)

    @pl.when(i == pl.num_programs(2) - 1)
    def _():
        dk[...] = turn(dka[...] * scale, ck[...], -sk[...]).astype(BF).reshape(dk.shape)
        dv[...] = dva[...].astype(BF).reshape(dv.shape)


def attention(joined, grad, cos, sin, pos, doc):
    half = 2 * BLK
    length = 2 * half
    joined = joined.reshape(2, 2, half, WIDE)
    grad = grad.reshape(2, 2, half, 2 * HD)
    part = lambda off: pl.BlockSpec(
        (None, None, BLK, HD), lambda s, h, i: (i // 2, s, i % 2, off + h)
    )
    whole = lambda off: pl.BlockSpec((2, None, half, HD), lambda s, h, i: (0, s, 0, off + h))
    tq = pl.BlockSpec((None, BLK, HD), lambda s, h, i: (s, i, 0))
    tk = pl.BlockSpec((None, length, HD), lambda s, h, i: (s, 0, 0))
    col = pl.BlockSpec((None, BLK, 1), lambda s, h, i: (s, i, 0))
    row = pl.BlockSpec((None, 1, length), lambda s, h, i: (s, 0, 0))
    results = call(
        attention_kernel,
        (2, 2, length // BLK),
        [part(0), whole(2), whole(4), part(0), tq, tq, tk, tk, col, col, row, row],
        [part(0), part(0), whole(0), whole(0)],
        [shape(2, 2, half, 2 * HD)] * 4,
        [
            pltpu.VMEM((length, HD), BF),
            pltpu.VMEM((length, HD), BF),
            pltpu.VMEM((length, HD), F32),
            pltpu.VMEM((length, HD), F32),
        ],
        flops=4 * length * length * HD * 14,
        traffic=4 * length * HD * 24,
        special=4 * length * length,
        scalars=0,
    )(
        joined, joined, joined, grad, cos, sin, cos, sin,
        pos[:, :, None], doc[:, :, None], pos[:, None, :], doc[:, None, :],
    )
    return [r.reshape(2 * length, 2 * HD) for r in results]


def column_plan(copies):
    units = FF // (16 * copies)
    for d in range(8):
        zl, x, core = d // 4, d // 2 % 2, d % 2
        for t in range(3):
            for m in range(2):
                head = core * 8 + zl * 4 + m * 2 + x
                yield 0, t * D + head * HD, HD, d, (t * 2 + m) * HD
        for zh in range(2):
            for y in range(copies):
                owner = (((zh * 2 + zl) * copies + y) * 2 + x) * 2 + core
                yield 1, owner * units, units, d, (zh * copies + y) * units


def deal_kernel(copies, wide, tall, wide_out, tall_out):
    pairs = ((wide, wide_out), (tall, tall_out))
    for which, start, width, d, at in column_plan(copies):
        source, target = pairs[which]
        target[d, :, at : at + width] = source[:, start : start + width]


def deal_columns(wide, tall, copies):
    rows = wide.shape[0]
    return call(
        functools.partial(deal_kernel, copies),
        (1,),
        [fixed(*wide.shape), fixed(*tall.shape)],
        [fixed(8, rows, WIDE), fixed(8, rows, UNITS)],
        [shape(8, rows, WIDE), shape(8, rows, UNITS)],
        traffic=rows * (3 * D + FF) * 4,
        scalars=0,
    )(wide, tall)


def collect_kernel(copies, which_one, source, target):
    for which, start, width, d, at in column_plan(copies):
        if which == which_one:
            target[:, start : start + width] = source[d, :, at : at + width].astype(F32)


def collect_columns(v, which, copies):
    rows, width = v.shape[1], (3 * D, FF)[which]
    return call(
        functools.partial(collect_kernel, copies, which),
        (1,),
        [fixed(*v.shape)],
        fixed(rows, width),
        shape(rows, width, dtype=F32),
        traffic=rows * width * 6,
        scalars=0,
    )(v)


def pack_kernel(*refs):
    for j, v in enumerate(refs[:-1]):
        refs[-1][j : j + 1, 0 : v.shape[1]] = v[...]


def pack_rows(vectors):
    vectors = [v[None] for v in vectors]
    return call(
        pack_kernel,
        (1,),
        [fixed(*v.shape) for v in vectors],
        fixed(len(vectors), BLK),
        shape(len(vectors), BLK),
        scalars=0,
    )(*vectors)


def swap(v, axes=("zl", "x", "core")):
    return lax.all_to_all(v, axes, 0, 0, tiled=True)


def gather_plain(v, split):
    return split(lax.all_gather(v, ("zh", "y"), axis=0, tiled=False))


def half_sum(v, other):
    return (v.astype(F32) + other.astype(F32)).astype(BF)


def split_rows(copies):
    def split(w):
        c = w.shape[-1]
        w = w.reshape(2, copies, 2, -1, c).transpose(0, 2, 1, 3, 4).reshape(2, 2, 2, BLK, c)
        return [w[a, :, b] for a in (0, 1) for b in (0, 1)]

    return split


def join_rows(copies):
    def join(w):
        c = w.shape[-1]
        w = w.reshape(2, 2, 2, BLK, c).transpose(0, 2, 1, 3, 4)
        w = w.reshape(2, 2, copies, -1, c).transpose(0, 2, 1, 3, 4)
        return w.reshape(2 * copies, -1, c)

    return join


def dense_parts(pieces):
    zh, y, core = (lax.axis_index(a) for a in ("zh", "y", "core"))
    w = jnp.stack(pieces).reshape(2, 2, HD // 2, D)
    w = jnp.where(y == 0, w, w[:, ::-1])
    same = zh == core
    return jnp.where(same, w[0], w[1]), jnp.where(same, w[1], w[0])


def dense_join(keep, other):
    first = lax.axis_index("core") == 0
    low, high = jnp.where(first, keep, other), jnp.where(first, other, keep)
    return jnp.stack([low, high], axis=1).reshape(2 * HD, D)


def dense_split(g):
    first = lax.axis_index("core") == 0
    g = g.reshape(2, 2, HD // 2, D)
    return jnp.where(first, g[:, 0], g[:, 1]), jnp.where(first, g[:, 1], g[:, 0])


def dense_sort(keep, other):
    same = lax.axis_index("zh") == lax.axis_index("core")
    w = jnp.stack([jnp.where(same, keep, other), jnp.where(same, other, keep)])
    return jnp.where(lax.axis_index("y") == 0, w, w[:, ::-1])


def gather_dense_plain(w):
    core, x = lax.axis_index("core"), lax.axis_index("x")
    w = lax.all_gather(w, ("zh", "y", "x", "core"), axis=0, tiled=True).reshape(2, 2, 2, HD, D)
    w = lax.dynamic_slice(w, (core, 0, x, 0, 0), (1, 2, 1, HD, D))
    return w.reshape(2 * HD, D)


def reduce_dense_plain(g):
    core, x = lax.axis_index("core"), lax.axis_index("x")
    w = jnp.zeros((2, 2, 2, HD, D), F32)
    g = g.astype(F32).reshape(1, 2, 1, HD, D)
    w = lax.dynamic_update_slice(w, g, (core, 0, x, 0, 0)).reshape(-1, D)
    return lax.psum_scatter(w, ("zh", "y", "x", "core"), scatter_dimension=0, tiled=True)


def shards(
    copies,
    block_input,
    output_grad,
    documents,
    span_order,
    attention_norm_gain,
    attention_norm_bias,
    query_key_value_weight,
    query_key_value_bias,
    dense_weight,
    dense_bias,
    mlp_norm_gain,
    mlp_norm_bias,
    to_hidden_weight,
    to_hidden_bias,
    from_hidden_weight,
    from_hidden_bias,
):
    span = block_input.shape[1]
    count = 16 * copies
    rows = D // count
    units = FF // count
    length = 4 * span
    zl, x, core = (lax.axis_index(a) for a in ("zl", "x", "core"))
    own_in, own_grad = block_input[0], output_grad[0]
    base = jnp.zeros((2,), jnp.int32)
    if copies == 2:
        base = base.at[0].set(lax.axis_index("zh") * 2 + lax.axis_index("y"))

    def spread_small(first):
        vectors = (
            first,
            attention_norm_bias,
            mlp_norm_gain,
            mlp_norm_bias,
            dense_bias,
            from_hidden_bias,
            query_key_value_bias,
            to_hidden_bias,
        )
        if copies == 2:
            small = pack_rows(vectors)
        else:
            small = jnp.stack([jnp.pad(v, (0, BLK - v.shape[0])) for v in vectors])
        facts = jnp.concatenate([documents[0], jnp.pad(span_order[0], (0, length - 4))])
        small = jnp.concatenate([small, facts.astype(BF).reshape(8, BLK)], axis=0)
        small = jnp.broadcast_to(small[None], (count, 16, BLK)).reshape(count * 16, BLK)
        return swap(small, AXES)

    def unpack(small):
        small = small.reshape(count, 16, BLK)
        row = (lax.axis_index("zh") * 2 * copies + lax.axis_index("y")) * 4
        facts = [lax.dynamic_slice(small, (row + s * copies * 4, 8, 0), (1, 8, BLK)) for s in (zl, 1 - zl)]
        facts = [v.astype(jnp.int32).reshape(2 * length) for v in facts]
        small = small[:, :8].astype(F32)
        take = lambda j, n: small[:, j, :n].reshape(-1)
        gains = jnp.stack([take(j, rows) for j in range(4)])
        out_shift = take(4, rows) + take(5, rows)
        joined_shift = take(6, 3 * rows).reshape(3, 2, 2, 2, 2, HD)
        joined_shift = lax.dynamic_slice(joined_shift, (0, core, zl, 0, x, 0), (3, 1, 1, 2, 1, HD))
        joined_shift = joined_shift.reshape(1, WIDE)
        hidden_shift = take(7, units).reshape(2, 2, copies, 2, 2, units)
        hidden_shift = lax.dynamic_slice(
            hidden_shift, (0, zl, 0, x, core, 0), (2, 1, copies, 1, 1, units)
        ).reshape(1, UNITS)

        offsets = jnp.arange(span, dtype=jnp.int32)
        pos, doc = [], []
        for known in facts:
            for c in (0, 1):
                for b in (0, 1):
                    block = (x ^ b) * 2 + (core ^ c)
                    doc.append(lax.dynamic_slice(known, (block * span,), (span,)))
                    pos.append(lax.dynamic_slice(known, (length + block,), (1,)) * span + offsets)
        pos = jnp.concatenate(pos).reshape(2, length)
        doc = jnp.concatenate(doc).reshape(2, length)
        inverse = jnp.power(THETA, -jnp.arange(ROT // 2, dtype=F32) * (2.0 / ROT))
        angles = pos.astype(F32)[:, :, None] * inverse
        cosine, sine = jnp.cos(angles), jnp.sin(angles)
        rest = jnp.zeros((2, length, HD - ROT), F32)
        cos_table = jnp.concatenate([cosine, cosine, rest + 1.0], axis=-1)
        sin_table = jnp.concatenate([-sine, sine, rest], axis=-1)


        return gains, out_shift, joined_shift, hidden_shift, pos, doc, cos_table, sin_table

    order = (3, 1, 2, 0)
    ordered = lambda v: [v[order.index(r)] for r in range(4)]
    halves = lambda v: (v[: v.shape[0] // 2], v[v.shape[0] // 2 :])
    join = lambda *v: jnp.concatenate(v, axis=0)
    block = lambda v, f: v[f * span : (f + 1) * span]
    low_sum = lambda v, w: (v.astype(F32) + w.astype(F32)).astype(BF)
    pair = copies == 2

    def near(d, own, names):
        return join(own, *[d[n] for n in names.split()])

    tasks, parts = {}, {}

    def once(name, make):
        if name not in parts:
            parts[name] = make()
        return parts[name]

    facts_of = lambda d: once("facts", lambda: unpack(d["ss"]))

    def move(name, axis, source):
        tasks[name] = (source, lambda v, d: flip(v, axis))

    def kernel(name, source, step):
        tasks[name] = (source, step)

    kernel(
        "deal",
        lambda d: query_key_value_weight,
        lambda v, d: deal_columns(v, to_hidden_weight, copies),
    )
    tasks["sw"] = (lambda d: d["deal"][0], lambda v, d: swap(v).reshape(2, 4 * rows, WIDE))
    tasks["st"] = (lambda d: d["deal"][1], lambda v, d: swap(v).reshape(2, 4 * rows, UNITS))
    tasks["ss"] = (lambda d: attention_norm_gain, lambda v, d: spread_small(v))
    chunk = jnp.concatenate([dense_weight, from_hidden_weight], axis=0)
    move("An", "y", lambda d: chunk)
    move("A0z", "zh", lambda d: halves(chunk)[0])
    move("A1z", "zh", lambda d: halves(chunk)[1])
    move("Af0", "y", lambda d: d["A0z"])
    move("Af1", "y", lambda d: d["A1z"])
    move("Wn", "y", lambda d: d["sw"])
    move("Wz", "zh", lambda d: d["sw"])
    move("Wf", "y", lambda d: d["Wz"])
    late = lambda v, d: after(v, d["A"][0])
    back_of = lambda d: [
        chunk,
        d["An"],
        join(late(d["A0z"], d), late(d["A1z"], d)),
        join(late(d["Af0"], d), late(d["Af1"], d)),
    ]
    back = lambda d: once("back", lambda: back_of(d))
    wide = lambda d: [d["sw"], d["Wn"], d["Wz"], d["Wf"]]
    tasks["Tg"] = (
        lambda d: d["st"],
        lambda v, d: lax.all_gather(v, ("zh", "y"), axis=0, tiled=False),
    )
    tasks["Br"] = (
        lambda d: d["B"],
        lambda v, d: lax.psum_scatter(v, ("zh", "y"), scatter_dimension=0, tiled=True),
    )
    tall_of = lambda d: d["Tg"] if pair else jnp.stack(split_rows(copies)(d["Tg"]))
    tall = lambda d: once("tall", lambda: tall_of(d))
    if not pair:
        back_of = lambda d: gather_plain(from_hidden_weight, lambda w: list(w.reshape(4, BLK, D)))
        wide = lambda d: once("wide", lambda: gather_plain(d["sw"], split_rows(copies)))
    dense_two_of = lambda d: dense_parts([p[:rows] for p in (chunk, d["An"], d["A0z"], d["Af0"])])
    dense_two = lambda d: once("dense_two", lambda: dense_two_of(d))
    move("dc", "core", lambda d: dense_two(d)[1])
    dense_of = lambda d: dense_join(dense_two(d)[0], d["dc"])
    dense = lambda d: once("dense", lambda: dense_of(d))
    if not pair:
        dense_of = lambda d: gather_dense_plain(dense_weight)

    for n, own in (("i", own_in), ("u", own_grad)):
        move(n + "x", "x", lambda d, own=own: own)
        move(n + "z", "zl", lambda d, own=own: own)
        move(n + "b", "x", lambda d, n=n: d[n + "z"])
        move(n + "0", "core", lambda d, own=own: own)
        move(n + "1", "core", lambda d, n=n: d[n + "x"])
        move(n + "2", "core", lambda d, n=n: d[n + "z"])
        move(n + "3", "core", lambda d, n=n: d[n + "b"])
    tokens_of = lambda d: (near(d, own_in, "ix iz ib"), join(*[d[n] for n in ("i0", "i1", "i2", "i3")]))
    tokens = lambda d: once("tokens", lambda: tokens_of(d))
    upstream_of = lambda d: (near(d, own_grad, "ux uz ub"), join(*[d[n] for n in ("u0", "u1", "u2", "u3")]))
    upstream = lambda d: once("upstream", lambda: upstream_of(d))

    kernel("norms", lambda d: facts_of(d)[0], lambda v, d: norms(*tokens(d), v))
    kernel("dO", lambda d: dense(d), lambda v, d: mixed_grad(*upstream(d), v))
    kernel(
        "joined",
        lambda d: d["norms"][0],
        lambda v, d: joined_product(base, v, wide(d), facts_of(d)[2]),
    )
    kernel(
        "A",
        lambda d: (d["joined"], d["dO"])[0],
        lambda v, d: attention(v, d["dO"], *[facts_of(d)[j] for j in (6, 7, 4, 5)]),
    )
    heads = lambda d: d["A"]
    kernel(
        "W",
        lambda d: d["norms"][0],
        lambda v, d: ordered(rows_grad(base, v, heads(d)[1:], order)),
    )
    kernel(
        "H",
        lambda d: d["norms"][1],
        lambda v, d: hidden_products(base, v, *upstream(d), tall(d), back(d), facts_of(d)[3]),
    )
    kernel(
        "T",
        lambda d: d["H"][1],
        lambda v, d: ordered(rows_grad(base, d["norms"][1], [v], order)),
    )
    kernel(
        "B", lambda d: d["H"][0], lambda v, d: units_grad(v, *upstream(d))
    )
    for h, n in ((1, "f"), (0, "n")):
        kernel(
            "P" + n,
            lambda d: d["H"][1],
            lambda v, d, h=h: pull_product(
                base, h, heads(d)[1:], v, tokens(d)[h], *d["norms"][2:], facts_of(d)[0], wide(d), tall(d)
            ),
        )
        kernel(
            "O" + n,
            lambda d: d["H"][0],
            lambda v, d, h=h: out_product(base, h, heads(d)[0], v, dense(d), back(d)),
        )

    def grad_dense(d):
        mixed, (near_up, far_up) = heads(d)[0], upstream(d)
        low, high = halves(mixed)
        return (dot(low, near_up, 0, 0) + dot(high, far_up, 0, 0)).astype(BF)

    g_dense = lambda d: once("g_dense", lambda: grad_dense(d))
    g_sort = lambda d: once("sort", lambda: dense_sort(dense_split(g_dense(d))[0], d["gd"]))
    for n in "WT":
        move(n + "3", "y", lambda d, n=n: d[n][3])
        move(n + "1", "y", lambda d, n=n: d[n][1])
    far_sum = lambda d, n: once(n + "far", lambda: low_sum(d[n][2], d[n + "3"]))
    move("zW", "zh", lambda d: far_sum(d, "W"))
    move("zT0", "zh", lambda d: halves(far_sum(d, "T"))[0])
    move("zT1", "zh", lambda d: halves(far_sum(d, "T"))[1])
    move("gd", "core", lambda d: dense_split(g_dense(d))[1])
    move("D1", "y", lambda d: g_sort(d)[:, 1])
    dense_y = lambda d: once("dense_y", lambda: g_sort(d)[:, 0].astype(F32) + d["D1"].astype(F32))
    move("zD", "zh", lambda d: dense_y(d)[1].astype(BF))
    add = lambda d, n, far: d[n][0].astype(F32) + d[n + "1"].astype(F32) + far.astype(F32)

    for n, k in (("p", "P"), ("o", "O")):
        part = lambda d, which, k=k: d[k + which][0] if k == "P" else d[k + which]
        total = lambda d, f, n=n, part=part: block(part(d, "n"), f).astype(F32) + d[f"{n}c{f}"].astype(F32)
        for f in range(4):
            move(f"{n}c{f}", "core", lambda d, f=f, part=part: block(part(d, "f"), f))
        move(n + "3", "x", lambda d, total=total: total(d, 3).astype(BF))
        move(n + "1", "x", lambda d, total=total: total(d, 1).astype(BF))
        move(
            n + "z",
            "zl",
            lambda d, n=n, total=total: (total(d, 2) + d[n + "3"].astype(F32)).astype(BF),
        )
        tasks[n] = lambda d, n=n, total=total: (
            total(d, 0) + d[n + "1"].astype(F32) + d[n + "z"].astype(F32)
        )

    grad_own = own_grad.astype(F32)

    def all_sums(v, w, hidden_sum):
        joined_sum = lax.dynamic_update_slice(
            jnp.zeros((3, 2, 2, 2, 2, HD), F32),
            (v[2] + w[2]).reshape(3, 1, 1, 2, 1, HD),
            (0, core, zl, 0, x, 0),
        )
        hidden_sum = lax.dynamic_update_slice(
            jnp.zeros((2, 2, copies, 2, 2, units), F32),
            hidden_sum.reshape(2, 1, copies, 1, 1, units),
            (0, zl, 0, x, core, 0),
        )
        sums = [*(v[1] + w[1]), jnp.sum(grad_own, axis=0), joined_sum, hidden_sum]
        return jnp.concatenate([s.reshape(count, -1) for s in sums], axis=1)

    tasks["gs"] = (
        lambda d: all_sums(d["Pn"], d["Pf"], d["H"][2]),
        lambda v, d: jnp.sum(swap(v, AXES), axis=0),
    )
    tasks["gw"] = (
        lambda d: add(d, "W", d["zW"]).astype(BF).reshape(8, rows, WIDE),
        lambda v, d: swap(v),
    )
    tasks["gt"] = (
        lambda d: add(d, "T", join(d["zT0"], d["zT1"])).astype(BF).reshape(8, rows, UNITS),
        lambda v, d: swap(v),
    )

    if pair:
        d = run(tasks)
        pull, out = tasks["p"](d), tasks["o"](d)
        sums, grad_wide, grad_tall = d["gs"], d["gw"], d["gt"]
        grad_dense = dense_y(d)[0] + d["zD"].astype(F32)
    else:
        names = [*CFG["y"], *CFG["zh"], "dc", "gd", "gw", "gt"]
        d = run(tasks, names)
        pull, out, sums = tasks["p"](d), tasks["o"](d), d["gs"]

        def scatter(pieces, plan):
            w = plan(jnp.stack(pieces).astype(F32))
            return lax.psum_scatter(w, ("zh", "y"), scatter_dimension=0, tiled=False)

        grad_wide = swap(scatter(d["W"], join_rows(copies)).astype(BF).reshape(8, rows, WIDE))
        grad_tall = swap(scatter(d["T"], join_rows(copies)).astype(BF).reshape(8, rows, UNITS))
        grad_dense = reduce_dense_plain(g_dense(d))

    grad_back = d["Br"].astype(F32)
    out_shift = facts_of(d)[1]
    grad_wide = collect_columns(grad_wide, 0, copies)
    grad_tall = collect_columns(grad_tall, 1, copies)

    own_wide = own_in.astype(F32)
    block_output = (own_wide + (out + out_shift)).astype(BF)[None]
    own_centre = own_wide - jnp.mean(own_wide, axis=-1, keepdims=True)
    own_spread = lax.rsqrt(jnp.mean(own_centre * own_centre, axis=-1, keepdims=True) + EPS)
    own_normal = own_centre * own_spread
    pull = own_spread * (
        pull
        - jnp.mean(pull, axis=-1, keepdims=True)
        - own_normal * jnp.mean(pull * own_normal, axis=-1, keepdims=True)
    )
    input_grad = (grad_own + pull).astype(BF)[None]

    cut = lambda a, n: sums[a : a + n]
    bias_sum = cut(4 * rows, rows)


    return (
        block_output,
        input_grad,
        cut(0, rows),
        cut(rows, rows),
        grad_wide,
        cut(5 * rows, 3 * rows),
        grad_dense,
        bias_sum,
        cut(2 * rows, rows),
        cut(3 * rows, rows),
        grad_tall,
        cut(8 * rows, units),
        grad_back,
        bias_sum,
    )


def solution(mesh):
    copies = mesh.shape["batch"] // 4
    inner = Mesh(mesh.devices.reshape(2, 2, copies, 2, 2), AXES)
    batch, ctx = AXES[:3], AXES[3:]
    tokens = P(batch, ctx, None)
    vector, matrix = P(AXES), P(AXES, None)
    params = (vector, vector, matrix, vector, matrix, vector)
    return jax.shard_map(
        functools.partial(shards, copies),
        mesh=inner,
        in_specs=(tokens, tokens, P(batch, None), P(batch, None)) + params + params,
        out_specs=(tokens, tokens) + params + params,
        check_vma=False,
    )
```

```python
import functools

import jax
import jax.numpy as jnp
from jax import lax
from jax.experimental import pallas as pl
from jax.experimental.pallas import tpu as pltpu
from jax.sharding import Mesh, PartitionSpec as P

D = 2048
H = 16
HD = 128
ROT = 32
FF = 8192
WIDE = 6 * HD
UNITS = FF // 8
BLK = 256
NBLK = D // BLK
EPS = 1e-05
NEG = -1e30
THETA = 10000.0
BF = jnp.bfloat16
F32 = jnp.float32
AXES = ("zh", "zl", "y", "x", "core")
VMEM = 50 * 2**20
COST = 1.0


CFG = {
    "swap": ["sw", "st", "ss", "gs", "gw", "gt"],
    "kernel": ["deal", "norms", "joined", "dO", "A", "W", "H", "T", "B", "Pf", "Pn", "Of", "On"],
    "x": ["ix", "ib", "ux", "ub", "p3", "p1", "o3", "o1"],
    "zl": ["iz", "uz", "pz", "oz"],
    "core": ["i0", "i1", "i2", "i3", "u0", "u1", "u2", "u3", "dc", "gd", "pc3", "pc1", "pc2", "pc0", "oc3", "oc1", "oc2", "oc0"],
    "y": ["An", "Wn", "Af0", "Wf", "Af1", "W3", "T3", "D1", "W1", "T1"],
    "zh": ["A0z", "Wz", "A1z", "zW", "zT0", "zT1", "zD"],
    "sc": ["Tg", "Br"],
    "depth": {"core": 3},
    "ties": {
        "T": ["W3"],
        "Pf": ["zW", "T3"],
        "Of": ["zT0"],
        "o3": ["W1", "gs"],
        "o1": ["zT1", "T1"],
        "oz": ["gw"],
    },
}


def after(v, *others):
    return lax.optimization_barrier((v, *others))[0]


def flip(v, axis):
    return lax.ppermute(v, axis, [(0, 1), (1, 0)])


def run(tasks, skip=()):
    channels = ("swap", "kernel", "x", "zl", "core", "y", "zh", "sc")
    lines = {c: [n for n in CFG[c] if n not in skip] for c in channels}
    done, at = {}, dict.fromkeys(lines, 0)
    first = lambda v: v[0] if isinstance(v, (list, tuple)) else v
    while any(at[c] < len(lines[c]) for c in lines):
        moved = False
        for c, names in lines.items():
            while at[c] < len(names):
                name = names[at[c]]
                source, step = tasks[name]
                waits = [w for w in CFG["ties"].get(name, ()) if w not in skip]
                place = at[c] - CFG["depth"].get(c, 1)
                if place >= 0:
                    waits.append(names[place])
                if any(w not in done for w in waits):
                    break
                try:
                    v = source(done)
                    if waits:
                        v = after(v, *[first(done[w]) for w in waits])
                    done[name] = step(v, done)
                except KeyError:
                    break
                at[c] += 1
                moved = True
        assert moved
    return done


def dot(a, b, ca, cb):
    return lax.dot_general(a, b, (((ca,), (cb,)), ((), ())), preferred_element_type=F32)


def call(kernel, grid, ins, outs, shapes, scratch=(), flops=0, traffic=0, special=0, scalars=1):
    return pl.pallas_call(
        kernel,
        grid_spec=pltpu.PrefetchScalarGridSpec(
            num_scalar_prefetch=scalars,
            grid=grid,
            in_specs=ins,
            out_specs=outs,
            scratch_shapes=scratch,
        ),
        out_shape=shapes,
        compiler_params=pltpu.CompilerParams(vmem_limit_bytes=VMEM),
        cost_estimate=pl.CostEstimate(
            flops=int(flops * COST), bytes_accessed=int(traffic * COST), transcendentals=int(special * COST)
        ),
    )


def shape(*dims, dtype=BF):
    return jax.ShapeDtypeStruct(dims, dtype)


def fixed(*dims):
    return pl.BlockSpec(dims, lambda *_: (0,) * len(dims))


def rows_of(width, rows=BLK):
    return pl.BlockSpec((rows, width), lambda i, *_: (i, 0))


def two_halves(width):
    return [
        pl.BlockSpec((BLK, width), lambda i, *_: (jnp.minimum(i, 3), 0)),
        pl.BlockSpec((BLK, width), lambda i, *_: (jnp.maximum(i - 4, 0), 0)),
    ]


def pick(near, far):
    return jnp.where(pl.program_id(0) < 4, near[...], far[...])


def place(base, r, p):
    s = r ^ base
    return (s // 2) * 4 + p * 2 + s % 2


def columns(index):
    return pl.ds(pl.multiple_of(index * BLK, BLK), BLK)


def norm_kernel(near, far, gains, one, two, mean, scale):
    v = pick(near, far).astype(F32)
    mu = jnp.mean(v, axis=-1, keepdims=True)
    v = v - mu
    r = lax.rsqrt(jnp.mean(v * v, axis=-1, keepdims=True) + EPS)
    v = v * r
    one[...] = (v * gains[0:1] + gains[1:2]).astype(BF)
    two[...] = (v * gains[2:3] + gains[3:4]).astype(BF)
    mean[...] = mu
    scale[...] = r


def norms(near, far, gains):
    n = 2 * near.shape[0]
    return call(
        norm_kernel,
        (n // BLK,),
        [*two_halves(D), fixed(4, D)],
        [rows_of(D), rows_of(D), rows_of(1), rows_of(1)],
        [shape(n, D), shape(n, D), shape(n, 1, dtype=F32), shape(n, 1, dtype=F32)],
        traffic=n * D * 6,
        flops=n * D * 10,
        scalars=0,
    )(near, far, gains)


def joined_kernel(base, v, w0, w1, w2, w3, shift, out):
    total = jnp.zeros((BLK, WIDE), F32) + shift[...]
    for r, w in enumerate((w0, w1, w2, w3)):
        for p in range(2):
            total += dot(v[:, columns(place(base[0], r, p))], w[p], 1, 0)
    out[...] = total


def joined_product(base, v, pieces, shift):
    n = v.shape[0]
    return call(
        joined_kernel,
        (n // BLK,),
        [rows_of(D), *[fixed(2, BLK, WIDE)] * 4, fixed(1, WIDE)],
        rows_of(WIDE),
        shape(n, WIDE, dtype=F32),
        flops=2 * n * D * WIDE,
        traffic=n * D * 2 + n * WIDE * 4 + D * WIDE * 2,
    )(base, v, *pieces, shift)


def mixed_grad_kernel(near, far, w, out):
    out[...] = dot(pick(near, far), w[...], 1, 1).astype(BF)


def mixed_grad(near, far, w):
    n, wide = 2 * near.shape[0], w.shape[0]
    return call(
        mixed_grad_kernel,
        (n // BLK,),
        [*two_halves(D), fixed(wide, D)],
        rows_of(wide),
        shape(n, wide),
        flops=2 * n * D * wide,
        traffic=n * D * 2,
        scalars=0,
    )(near, far, w)


def hidden_kernel(
    skip, base, v, near, far, w, b0, b1, b2, b3, shift, active, grad, sums, back
):
    up = pick(near, far)
    for r, b in enumerate((b0, b1, b2, b3)):
        back[:, columns(r ^ base[0])] = dot(up, b[skip:], 1, 1)
    u = jnp.zeros((BLK, UNITS), F32) + shift[...]
    for r in range(4):
        for p in range(2):
            u += dot(v[:, columns(place(base[1], r, p))], w[r, p], 1, 0)
    below = 0.5 * (1.0 + lax.erf(u * (0.5**0.5)))
    active[...] = (u * below).astype(BF)
    slope = below + u * jnp.exp(-0.5 * u * u) * ((2.0 * jnp.pi) ** (-0.5))
    low = (back[...] * slope).astype(BF)
    grad[...] = low

    @pl.when(pl.program_id(0) == 0)
    def _():
        sums[...] = jnp.zeros_like(sums)

    sums[...] += jnp.sum(low.astype(F32), axis=0, keepdims=True)


def hidden_products(base, v, near, far, pieces, back_pieces, shift):
    n, tall = v.shape[0], back_pieces[0].shape[0]
    return call(
        functools.partial(hidden_kernel, tall - BLK),
        (n // BLK,),
        [rows_of(D), *two_halves(D), fixed(4, 2, BLK, UNITS), *[fixed(tall, D)] * 4, fixed(1, UNITS)],
        [rows_of(UNITS), rows_of(UNITS), fixed(1, UNITS)],
        [shape(n, UNITS), shape(n, UNITS), shape(1, UNITS, dtype=F32)],
        [pltpu.VMEM((BLK, UNITS), F32)],
        flops=4 * n * D * UNITS,
        traffic=n * D * 4 + n * UNITS * 4 + D * UNITS * 4,
        special=2 * n * UNITS,
    )(base, v, near, far, pieces, *back_pieces, shift)


def out_kernel(skip, base, mixed, active, w, b0, b1, b2, b3, out):
    total = dot(mixed[...], w[...], 1, 0)
    for r, b in enumerate((b0, b1, b2, b3)):
        total += dot(active[:, columns(r ^ base[0])], b[skip:], 1, 0)
    out[...] = total.astype(BF)


def out_product(base, half, mixed, active, dense_w, back_pieces):
    n, tall = mixed.shape[0] // 2, back_pieces[0].shape[0]
    steps = n // BLK
    half_rows = lambda width: pl.BlockSpec((BLK, width), lambda i, *_: (i + half * steps, 0))
    return call(
        functools.partial(out_kernel, tall - BLK),
        (steps,),
        [half_rows(2 * HD), half_rows(UNITS), fixed(2 * HD, D), *[fixed(tall, D)] * 4],
        rows_of(D),
        shape(n, D),
        flops=2 * n * D * (UNITS + 2 * HD),
        traffic=n * D * 2 + n * UNITS * 2 + D * UNITS * 2,
    )(base, mixed, active, dense_w, *back_pieces)


def pull_kernel(
    base, dq, dk, dv, du, tokens, mean, scale, gains, q0, q1, q2, q3, w, out, sums, wide, held
):
    @pl.when(pl.program_id(0) == 0)
    def _():
        sums[...] = jnp.zeros_like(sums)
        wide[...] = jnp.zeros_like(wide)

    add = lambda v: jnp.sum(v, axis=0, keepdims=True)
    for t, v in enumerate((dq, dk, dv)):
        wide[:, 2 * HD * t : 2 * HD * (t + 1)] += add(v[...].astype(F32))
    for r, q in enumerate((q0, q1, q2, q3)):
        for p in range(2):
            at = columns(place(base[0], r, p))
            one = (
                dot(dq[...], q[p, :, 0 : 2 * HD], 1, 1)
                + dot(dk[...], q[p, :, 2 * HD : 4 * HD], 1, 1)
                + dot(dv[...], q[p, :, 4 * HD :], 1, 1)
            )
            normal = (tokens[:, at].astype(F32) - mean[...]) * scale[...]
            sums[0:1, at] += add(one * normal)
            sums[1:2, at] += add(one)
            held[:, at] = one * gains[0:1, at]
    for r in range(4):
        for p in range(2):
            at = columns(place(base[1], r, p))
            two = dot(du[...], w[r, p], 1, 1)
            normal = (tokens[:, at].astype(F32) - mean[...]) * scale[...]
            sums[2:3, at] += add(two * normal)
            sums[3:4, at] += add(two)
            out[:, at] = (held[:, at] + two * gains[2:3, at]).astype(BF)


def pull_product(base, half, grads, du, tokens, mean, scale, gains, joined_pieces, pieces):
    n = du.shape[0] // 2
    steps = n // BLK
    half_rows = lambda width: pl.BlockSpec((BLK, width), lambda i, *_: (i + half * steps, 0))
    return call(
        pull_kernel,
        (steps,),
        [
            *[half_rows(2 * HD)] * 3,
            half_rows(UNITS),
            rows_of(D),
            half_rows(1),
            half_rows(1),
            fixed(4, D),
            *[fixed(2, BLK, WIDE)] * 4,
            fixed(4, 2, BLK, UNITS),
        ],
        [rows_of(D), fixed(4, D), fixed(1, WIDE)],
        [shape(n, D), shape(4, D, dtype=F32), shape(1, WIDE, dtype=F32)],
        [pltpu.VMEM((BLK, D), F32)],
        flops=2 * n * D * (UNITS + WIDE),
        traffic=n * D * 4 + n * UNITS * 4 + D * (UNITS + WIDE) * 2,
    )(base, *grads, du, tokens, mean, scale, gains, *joined_pieces, pieces)


def rows_grad_kernel(count, base, v, *refs):
    rights, outs = refs[:count], refs[count:]
    step = pl.program_id(0)
    v = v[...]
    parts, width = [], 0
    for right in rights:
        parts.append(dot(v, right[...], 0, 0).astype(BF))
    for j, out in enumerate(outs):

        @pl.when(step // 2 == j)
        def _(out=out):
            at = 0
            for part in parts:
                out[:, at : at + part.shape[1]] = part
                at += part.shape[1]


def rows_grad(base, v, rights, order):
    n, width = v.shape[0], sum(r.shape[1] for r in rights)

    def chosen(i, b):
        r = sum(jnp.where(i // 2 == j, r, 0) for j, r in enumerate(order))
        return (0, place(b[0], r, i % 2))

    def slot(j):
        return pl.BlockSpec((BLK, width), lambda i, b: (jnp.clip(i - 2 * j, 0, 1), 0))

    return call(
        functools.partial(rows_grad_kernel, len(rights)),
        (2 * len(order),),
        [pl.BlockSpec((n, BLK), chosen), *[fixed(*r.shape) for r in rights]],
        [slot(j) for j in range(len(order))],
        [shape(2 * BLK, width)] * len(order),
        flops=2 * n * BLK * 2 * len(order) * width,
        traffic=n * width * 2 + n * BLK * 4 * len(order),
    )(base, v, *rights)


def units_grad_kernel(v, near, far, out):
    n = near.shape[0]
    out[...] = (dot(v[:n], near[...], 0, 0) + dot(v[n:], far[...], 0, 0)).astype(BF)


def units_grad(v, near, far):
    n = v.shape[0]
    return call(
        units_grad_kernel,
        (UNITS // BLK,),
        [pl.BlockSpec((n, BLK), lambda i: (0, i)), fixed(n // 2, D), fixed(n // 2, D)],
        rows_of(D),
        shape(UNITS, D),
        flops=2 * n * UNITS * D,
        traffic=n * D * 2 + (n + D) * UNITS * 2,
        scalars=0,
    )(v, near, far)


def turn(v, cos, sin):
    lane = lax.broadcasted_iota(jnp.int32, v.shape, 1)
    half = ROT // 2
    swapped = jnp.where(lane < half, pltpu.roll(v, HD - half, 1), pltpu.roll(v, half, 1))
    return v * cos + swapped * sin


def attention_kernel(
    q, k, v, do, cq, sq, ck, sk, pq, eq, pk, ek, o, dq, dk, dv, ks, vs, dka, dva
):
    i = pl.program_id(2)
    scale = HD ** (-0.5)
    flat = lambda a: a.reshape(-1, HD)

    @pl.when(i == 0)
    def _():
        ks[...] = turn(flat(k[...]), ck[...], sk[...]).astype(BF)
        vs[...] = flat(v[...]).astype(BF)
        dka[...] = jnp.zeros_like(dka)
        dva[...] = jnp.zeros_like(dva)

    qr = turn(q[...], cq[...], sq[...]).astype(BF)
    s = dot(qr, ks[...], 1, 1) * scale
    allowed = (pk[...] <= pq[...]) & (ek[...] == eq[...])
    s = jnp.where(allowed, s, NEG)
    e = jnp.exp(s - jnp.max(s, axis=-1, keepdims=True))
    p = e / jnp.sum(e, axis=-1, keepdims=True)
    low = p.astype(BF)
    o[...] = dot(low, vs[...], 1, 0).astype(BF)
    dp = dot(do[...], vs[...], 1, 1)
    ds = (p * (dp - jnp.sum(p * dp, axis=-1, keepdims=True))).astype(BF)
    dq[...] = turn(dot(ds, ks[...], 1, 0) * scale, cq[...], -sq[...]).astype(BF)
    dva[...] += dot(low, do[...], 0, 0)
    dka[...] += dot(ds, qr, 0, 0)

    @pl.when(i == pl.num_programs(2) - 1)
    def _():
        dk[...] = turn(dka[...] * scale, ck[...], -sk[...]).astype(BF).reshape(dk.shape)
        dv[...] = dva[...].astype(BF).reshape(dv.shape)


def attention(joined, grad, cos, sin, pos, doc):
    half = 2 * BLK
    length = 2 * half
    joined = joined.reshape(2, 2, half, WIDE)
    grad = grad.reshape(2, 2, half, 2 * HD)
    part = lambda off: pl.BlockSpec(
        (None, None, BLK, HD), lambda s, h, i: (i // 2, s, i % 2, off + h)
    )
    whole = lambda off: pl.BlockSpec((2, None, half, HD), lambda s, h, i: (0, s, 0, off + h))
    tq = pl.BlockSpec((None, BLK, HD), lambda s, h, i: (s, i, 0))
    tk = pl.BlockSpec((None, length, HD), lambda s, h, i: (s, 0, 0))
    col = pl.BlockSpec((None, BLK, 1), lambda s, h, i: (s, i, 0))
    row = pl.BlockSpec((None, 1, length), lambda s, h, i: (s, 0, 0))
    results = call(
        attention_kernel,
        (2, 2, length // BLK),
        [part(0), whole(2), whole(4), part(0), tq, tq, tk, tk, col, col, row, row],
        [part(0), part(0), whole(0), whole(0)],
        [shape(2, 2, half, 2 * HD)] * 4,
        [
            pltpu.VMEM((length, HD), BF),
            pltpu.VMEM((length, HD), BF),
            pltpu.VMEM((length, HD), F32),
            pltpu.VMEM((length, HD), F32),
        ],
        flops=4 * length * length * HD * 14,
        traffic=4 * length * HD * 24,
        special=4 * length * length,
        scalars=0,
    )(
        joined, joined, joined, grad, cos, sin, cos, sin,
        pos[:, :, None], doc[:, :, None], pos[:, None, :], doc[:, None, :],
    )
    return [r.reshape(2 * length, 2 * HD) for r in results]


def column_plan(copies):
    units = FF // (16 * copies)
    for d in range(8):
        zl, x, core = d // 4, d // 2 % 2, d % 2
        for t in range(3):
            for m in range(2):
                head = core * 8 + zl * 4 + m * 2 + x
                yield 0, t * D + head * HD, HD, d, (t * 2 + m) * HD
        for zh in range(2):
            for y in range(copies):
                owner = (((zh * 2 + zl) * copies + y) * 2 + x) * 2 + core
                yield 1, owner * units, units, d, (zh * copies + y) * units


def deal_kernel(copies, wide, tall, wide_out, tall_out):
    pairs = ((wide, wide_out), (tall, tall_out))
    for which, start, width, d, at in column_plan(copies):
        source, target = pairs[which]
        target[d, :, at : at + width] = source[:, start : start + width]


def deal_columns(wide, tall, copies):
    rows = wide.shape[0]
    return call(
        functools.partial(deal_kernel, copies),
        (1,),
        [fixed(*wide.shape), fixed(*tall.shape)],
        [fixed(8, rows, WIDE), fixed(8, rows, UNITS)],
        [shape(8, rows, WIDE), shape(8, rows, UNITS)],
        traffic=rows * (3 * D + FF) * 4,
        scalars=0,
    )(wide, tall)


def collect_kernel(copies, which_one, source, target):
    for which, start, width, d, at in column_plan(copies):
        if which == which_one:
            target[:, start : start + width] = source[d, :, at : at + width].astype(F32)


def collect_columns(v, which, copies):
    rows, width = v.shape[1], (3 * D, FF)[which]
    return call(
        functools.partial(collect_kernel, copies, which),
        (1,),
        [fixed(*v.shape)],
        fixed(rows, width),
        shape(rows, width, dtype=F32),
        traffic=rows * width * 6,
        scalars=0,
    )(v)


def pack_kernel(*refs):
    for j, v in enumerate(refs[:-1]):
        refs[-1][j : j + 1, 0 : v.shape[1]] = v[...]


def pack_rows(vectors):
    vectors = [v[None] for v in vectors]
    return call(
        pack_kernel,
        (1,),
        [fixed(*v.shape) for v in vectors],
        fixed(len(vectors), BLK),
        shape(len(vectors), BLK),
        scalars=0,
    )(*vectors)


def swap(v, axes=("zl", "x", "core")):
    return lax.all_to_all(v, axes, 0, 0, tiled=True)


def gather_plain(v, split):
    return split(lax.all_gather(v, ("zh", "y"), axis=0, tiled=False))


def half_sum(v, other):
    return (v.astype(F32) + other.astype(F32)).astype(BF)


def split_rows(copies):
    def split(w):
        c = w.shape[-1]
        w = w.reshape(2, copies, 2, -1, c).transpose(0, 2, 1, 3, 4).reshape(2, 2, 2, BLK, c)
        return [w[a, :, b] for a in (0, 1) for b in (0, 1)]

    return split


def join_rows(copies):
    def join(w):
        c = w.shape[-1]
        w = w.reshape(2, 2, 2, BLK, c).transpose(0, 2, 1, 3, 4)
        w = w.reshape(2, 2, copies, -1, c).transpose(0, 2, 1, 3, 4)
        return w.reshape(2 * copies, -1, c)

    return join


def dense_parts(pieces):
    zh, y, core = (lax.axis_index(a) for a in ("zh", "y", "core"))
    w = jnp.stack(pieces).reshape(2, 2, HD // 2, D)
    w = jnp.where(y == 0, w, w[:, ::-1])
    same = zh == core
    return jnp.where(same, w[0], w[1]), jnp.where(same, w[1], w[0])


def dense_join(keep, other):
    first = lax.axis_index("core") == 0
    low, high = jnp.where(first, keep, other), jnp.where(first, other, keep)
    return jnp.stack([low, high], axis=1).reshape(2 * HD, D)


def dense_split(g):
    first = lax.axis_index("core") == 0
    g = g.reshape(2, 2, HD // 2, D)
    return jnp.where(first, g[:, 0], g[:, 1]), jnp.where(first, g[:, 1], g[:, 0])


def dense_sort(keep, other):
    same = lax.axis_index("zh") == lax.axis_index("core")
    w = jnp.stack([jnp.where(same, keep, other), jnp.where(same, other, keep)])
    return jnp.where(lax.axis_index("y") == 0, w, w[:, ::-1])


def gather_dense_plain(w):
    core, x = lax.axis_index("core"), lax.axis_index("x")
    w = lax.all_gather(w, ("zh", "y", "x", "core"), axis=0, tiled=True).reshape(2, 2, 2, HD, D)
    w = lax.dynamic_slice(w, (core, 0, x, 0, 0), (1, 2, 1, HD, D))
    return w.reshape(2 * HD, D)


def reduce_dense_plain(g):
    core, x = lax.axis_index("core"), lax.axis_index("x")
    w = jnp.zeros((2, 2, 2, HD, D), F32)
    g = g.astype(F32).reshape(1, 2, 1, HD, D)
    w = lax.dynamic_update_slice(w, g, (core, 0, x, 0, 0)).reshape(-1, D)
    return lax.psum_scatter(w, ("zh", "y", "x", "core"), scatter_dimension=0, tiled=True)


def shards(
    copies,
    block_input,
    output_grad,
    documents,
    span_order,
    attention_norm_gain,
    attention_norm_bias,
    query_key_value_weight,
    query_key_value_bias,
    dense_weight,
    dense_bias,
    mlp_norm_gain,
    mlp_norm_bias,
    to_hidden_weight,
    to_hidden_bias,
    from_hidden_weight,
    from_hidden_bias,
):
    span = block_input.shape[1]
    count = 16 * copies
    rows = D // count
    units = FF // count
    length = 4 * span
    zl, x, core = (lax.axis_index(a) for a in ("zl", "x", "core"))
    own_in, own_grad = block_input[0], output_grad[0]
    base = jnp.zeros((2,), jnp.int32)
    if copies == 2:
        base = base.at[0].set(lax.axis_index("zh") * 2 + lax.axis_index("y"))

    def spread_small(first):
        vectors = (
            first,
            attention_norm_bias,
            mlp_norm_gain,
            mlp_norm_bias,
            dense_bias,
            from_hidden_bias,
            query_key_value_bias,
            to_hidden_bias,
        )
        if copies == 2:
            small = pack_rows(vectors)
        else:
            small = jnp.stack([jnp.pad(v, (0, BLK - v.shape[0])) for v in vectors])
        facts = jnp.concatenate([documents[0], jnp.pad(span_order[0], (0, length - 4))])
        small = jnp.concatenate([small, facts.astype(BF).reshape(8, BLK)], axis=0)
        small = jnp.broadcast_to(small[None], (count, 16, BLK)).reshape(count * 16, BLK)
        return swap(small, AXES)

    def unpack(small):
        small = small.reshape(count, 16, BLK)
        row = (lax.axis_index("zh") * 2 * copies + lax.axis_index("y")) * 4
        facts = [lax.dynamic_slice(small, (row + s * copies * 4, 8, 0), (1, 8, BLK)) for s in (zl, 1 - zl)]
        facts = [v.astype(jnp.int32).reshape(2 * length) for v in facts]
        small = small[:, :8].astype(F32)
        take = lambda j, n: small[:, j, :n].reshape(-1)
        gains = jnp.stack([take(j, rows) for j in range(4)])
        out_shift = take(4, rows) + take(5, rows)
        joined_shift = take(6, 3 * rows).reshape(3, 2, 2, 2, 2, HD)
        joined_shift = lax.dynamic_slice(joined_shift, (0, core, zl, 0, x, 0), (3, 1, 1, 2, 1, HD))
        joined_shift = joined_shift.reshape(1, WIDE)
        hidden_shift = take(7, units).reshape(2, 2, copies, 2, 2, units)
        hidden_shift = lax.dynamic_slice(
            hidden_shift, (0, zl, 0, x, core, 0), (2, 1, copies, 1, 1, units)
        ).reshape(1, UNITS)

        offsets = jnp.arange(span, dtype=jnp.int32)
        pos, doc = [], []
        for known in facts:
            for c in (0, 1):
                for b in (0, 1):
                    block = (x ^ b) * 2 + (core ^ c)
                    doc.append(lax.dynamic_slice(known, (block * span,), (span,)))
                    pos.append(lax.dynamic_slice(known, (length + block,), (1,)) * span + offsets)
        pos = jnp.concatenate(pos).reshape(2, length)
        doc = jnp.concatenate(doc).reshape(2, length)
        inverse = jnp.power(THETA, -jnp.arange(ROT // 2, dtype=F32) * (2.0 / ROT))
        angles = pos.astype(F32)[:, :, None] * inverse
        cosine, sine = jnp.cos(angles), jnp.sin(angles)
        rest = jnp.zeros((2, length, HD - ROT), F32)
        cos_table = jnp.concatenate([cosine, cosine, rest + 1.0], axis=-1)
        sin_table = jnp.concatenate([-sine, sine, rest], axis=-1)


        return gains, out_shift, joined_shift, hidden_shift, pos, doc, cos_table, sin_table

    order = (3, 1, 2, 0)
    ordered = lambda v: [v[order.index(r)] for r in range(4)]
    halves = lambda v: (v[: v.shape[0] // 2], v[v.shape[0] // 2 :])
    join = lambda *v: jnp.concatenate(v, axis=0)
    block = lambda v, f: v[f * span : (f + 1) * span]
    low_sum = lambda v, w: (v.astype(F32) + w.astype(F32)).astype(BF)
    pair = copies == 2

    def near(d, own, names):
        return join(own, *[d[n] for n in names.split()])

    tasks, parts = {}, {}

    def once(name, make):
        if name not in parts:
            parts[name] = make()
        return parts[name]

    facts_of = lambda d: once("facts", lambda: unpack(d["ss"]))

    def move(name, axis, source):
        tasks[name] = (source, lambda v, d: flip(v, axis))

    def kernel(name, source, step):
        tasks[name] = (source, step)

    kernel(
        "deal",
        lambda d: query_key_value_weight,
        lambda v, d: deal_columns(v, to_hidden_weight, copies),
    )
    tasks["sw"] = (lambda d: d["deal"][0], lambda v, d: swap(v).reshape(2, 4 * rows, WIDE))
    tasks["st"] = (lambda d: d["deal"][1], lambda v, d: swap(v).reshape(2, 4 * rows, UNITS))
    tasks["ss"] = (lambda d: attention_norm_gain, lambda v, d: spread_small(v))
    chunk = jnp.concatenate([dense_weight, from_hidden_weight], axis=0)
    move("An", "y", lambda d: chunk)
    move("A0z", "zh", lambda d: halves(chunk)[0])
    move("A1z", "zh", lambda d: halves(chunk)[1])
    move("Af0", "y", lambda d: d["A0z"])
    move("Af1", "y", lambda d: d["A1z"])
    move("Wn", "y", lambda d: d["sw"])
    move("Wz", "zh", lambda d: d["sw"])
    move("Wf", "y", lambda d: d["Wz"])
    late = lambda v, d: after(v, d["A"][0])
    back_of = lambda d: [
        chunk,
        d["An"],
        join(late(d["A0z"], d), late(d["A1z"], d)),
        join(late(d["Af0"], d), late(d["Af1"], d)),
    ]
    back = lambda d: once("back", lambda: back_of(d))
    wide = lambda d: [d["sw"], d["Wn"], d["Wz"], d["Wf"]]
    tasks["Tg"] = (
        lambda d: d["st"],
        lambda v, d: lax.all_gather(v, ("zh", "y"), axis=0, tiled=False),
    )
    tasks["Br"] = (
        lambda d: d["B"],
        lambda v, d: lax.psum_scatter(v, ("zh", "y"), scatter_dimension=0, tiled=True),
    )
    tall_of = lambda d: d["Tg"] if pair else jnp.stack(split_rows(copies)(d["Tg"]))
    tall = lambda d: once("tall", lambda: tall_of(d))
    if not pair:
        back_of = lambda d: gather_plain(from_hidden_weight, lambda w: list(w.reshape(4, BLK, D)))
        wide = lambda d: once("wide", lambda: gather_plain(d["sw"], split_rows(copies)))
    dense_two_of = lambda d: dense_parts([p[:rows] for p in (chunk, d["An"], d["A0z"], d["Af0"])])
    dense_two = lambda d: once("dense_two", lambda: dense_two_of(d))
    move("dc", "core", lambda d: dense_two(d)[1])
    dense_of = lambda d: dense_join(dense_two(d)[0], d["dc"])
    dense = lambda d: once("dense", lambda: dense_of(d))
    if not pair:
        dense_of = lambda d: gather_dense_plain(dense_weight)

    for n, own in (("i", own_in), ("u", own_grad)):
        move(n + "x", "x", lambda d, own=own: own)
        move(n + "z", "zl", lambda d, own=own: own)
        move(n + "b", "x", lambda d, n=n: d[n + "z"])
        move(n + "0", "core", lambda d, own=own: own)
        move(n + "1", "core", lambda d, n=n: d[n + "x"])
        move(n + "2", "core", lambda d, n=n: d[n + "z"])
        move(n + "3", "core", lambda d, n=n: d[n + "b"])
    tokens_of = lambda d: (near(d, own_in, "ix iz ib"), join(*[d[n] for n in ("i0", "i1", "i2", "i3")]))
    tokens = lambda d: once("tokens", lambda: tokens_of(d))
    upstream_of = lambda d: (near(d, own_grad, "ux uz ub"), join(*[d[n] for n in ("u0", "u1", "u2", "u3")]))
    upstream = lambda d: once("upstream", lambda: upstream_of(d))

    kernel("norms", lambda d: facts_of(d)[0], lambda v, d: norms(*tokens(d), v))
    kernel("dO", lambda d: dense(d), lambda v, d: mixed_grad(*upstream(d), v))
    kernel(
        "joined",
        lambda d: d["norms"][0],
        lambda v, d: joined_product(base, v, wide(d), facts_of(d)[2]),
    )
    kernel(
        "A",
        lambda d: (d["joined"], d["dO"])[0],
        lambda v, d: attention(v, d["dO"], *[facts_of(d)[j] for j in (6, 7, 4, 5)]),
    )
    heads = lambda d: d["A"]
    kernel(
        "W",
        lambda d: d["norms"][0],
        lambda v, d: ordered(rows_grad(base, v, heads(d)[1:], order)),
    )
    kernel(
        "H",
        lambda d: d["norms"][1],
        lambda v, d: hidden_products(base, v, *upstream(d), tall(d), back(d), facts_of(d)[3]),
    )
    kernel(
        "T",
        lambda d: d["H"][1],
        lambda v, d: ordered(rows_grad(base, d["norms"][1], [v], order)),
    )
    kernel(
        "B", lambda d: d["H"][0], lambda v, d: units_grad(v, *upstream(d))
    )
    for h, n in ((1, "f"), (0, "n")):
        kernel(
            "P" + n,
            lambda d: d["H"][1],
            lambda v, d, h=h: pull_product(
                base, h, heads(d)[1:], v, tokens(d)[h], *d["norms"][2:], facts_of(d)[0], wide(d), tall(d)
            ),
        )
        kernel(
            "O" + n,
            lambda d: d["H"][0],
            lambda v, d, h=h: out_product(base, h, heads(d)[0], v, dense(d), back(d)),
        )

    def grad_dense(d):
        mixed, (near_up, far_up) = heads(d)[0], upstream(d)
        low, high = halves(mixed)
        return (dot(low, near_up, 0, 0) + dot(high, far_up, 0, 0)).astype(BF)

    g_dense = lambda d: once("g_dense", lambda: grad_dense(d))
    g_sort = lambda d: once("sort", lambda: dense_sort(dense_split(g_dense(d))[0], d["gd"]))
    for n in "WT":
        move(n + "3", "y", lambda d, n=n: d[n][3])
        move(n + "1", "y", lambda d, n=n: d[n][1])
    far_sum = lambda d, n: once(n + "far", lambda: low_sum(d[n][2], d[n + "3"]))
    move("zW", "zh", lambda d: far_sum(d, "W"))
    move("zT0", "zh", lambda d: halves(far_sum(d, "T"))[0])
    move("zT1", "zh", lambda d: halves(far_sum(d, "T"))[1])
    move("gd", "core", lambda d: dense_split(g_dense(d))[1])
    move("D1", "y", lambda d: g_sort(d)[:, 1])
    dense_y = lambda d: once("dense_y", lambda: g_sort(d)[:, 0].astype(F32) + d["D1"].astype(F32))
    move("zD", "zh", lambda d: dense_y(d)[1].astype(BF))
    add = lambda d, n, far: d[n][0].astype(F32) + d[n + "1"].astype(F32) + far.astype(F32)

    for n, k in (("p", "P"), ("o", "O")):
        part = lambda d, which, k=k: d[k + which][0] if k == "P" else d[k + which]
        total = lambda d, f, n=n, part=part: block(part(d, "n"), f).astype(F32) + d[f"{n}c{f}"].astype(F32)
        for f in range(4):
            move(f"{n}c{f}", "core", lambda d, f=f, part=part: block(part(d, "f"), f))
        move(n + "3", "x", lambda d, total=total: total(d, 3).astype(BF))
        move(n + "1", "x", lambda d, total=total: total(d, 1).astype(BF))
        move(
            n + "z",
            "zl",
            lambda d, n=n, total=total: (total(d, 2) + d[n + "3"].astype(F32)).astype(BF),
        )
        tasks[n] = lambda d, n=n, total=total: (
            total(d, 0) + d[n + "1"].astype(F32) + d[n + "z"].astype(F32)
        )

    grad_own = own_grad.astype(F32)

    def all_sums(v, w, hidden_sum):
        joined_sum = lax.dynamic_update_slice(
            jnp.zeros((3, 2, 2, 2, 2, HD), F32),
            (v[2] + w[2]).reshape(3, 1, 1, 2, 1, HD),
            (0, core, zl, 0, x, 0),
        )
        hidden_sum = lax.dynamic_update_slice(
            jnp.zeros((2, 2, copies, 2, 2, units), F32),
            hidden_sum.reshape(2, 1, copies, 1, 1, units),
            (0, zl, 0, x, core, 0),
        )
        sums = [*(v[1] + w[1]), jnp.sum(grad_own, axis=0), joined_sum, hidden_sum]
        return jnp.concatenate([s.reshape(count, -1) for s in sums], axis=1)

    tasks["gs"] = (
        lambda d: all_sums(d["Pn"], d["Pf"], d["H"][2]),
        lambda v, d: jnp.sum(swap(v, AXES), axis=0),
    )
    tasks["gw"] = (
        lambda d: add(d, "W", d["zW"]).astype(BF).reshape(8, rows, WIDE),
        lambda v, d: swap(v),
    )
    tasks["gt"] = (
        lambda d: add(d, "T", join(d["zT0"], d["zT1"])).astype(BF).reshape(8, rows, UNITS),
        lambda v, d: swap(v),
    )

    if pair:
        d = run(tasks)
        pull, out = tasks["p"](d), tasks["o"](d)
        sums, grad_wide, grad_tall = d["gs"], d["gw"], d["gt"]
        grad_dense = dense_y(d)[0] + d["zD"].astype(F32)
    else:
        names = [*CFG["y"], *CFG["zh"], "dc", "gd", "gw", "gt"]
        d = run(tasks, names)
        pull, out, sums = tasks["p"](d), tasks["o"](d), d["gs"]

        def scatter(pieces, plan):
            w = plan(jnp.stack(pieces).astype(F32))
            return lax.psum_scatter(w, ("zh", "y"), scatter_dimension=0, tiled=False)

        grad_wide = swap(scatter(d["W"], join_rows(copies)).astype(BF).reshape(8, rows, WIDE))
        grad_tall = swap(scatter(d["T"], join_rows(copies)).astype(BF).reshape(8, rows, UNITS))
        grad_dense = reduce_dense_plain(g_dense(d))

    grad_back = d["Br"].astype(F32)
    out_shift = facts_of(d)[1]
    grad_wide = collect_columns(grad_wide, 0, copies)
    grad_tall = collect_columns(grad_tall, 1, copies)

    own_wide = own_in.astype(F32)
    block_output = (own_wide + (out + out_shift)).astype(BF)[None]
    own_centre = own_wide - jnp.mean(own_wide, axis=-1, keepdims=True)
    own_spread = lax.rsqrt(jnp.mean(own_centre * own_centre, axis=-1, keepdims=True) + EPS)
    own_normal = own_centre * own_spread
    pull = own_spread * (
        pull
        - jnp.mean(pull, axis=-1, keepdims=True)
        - own_normal * jnp.mean(pull * own_normal, axis=-1, keepdims=True)
    )
    input_grad = (grad_own + pull).astype(BF)[None]

    cut = lambda a, n: sums[a : a + n]
    bias_sum = cut(4 * rows, rows)


    return (
        block_output,
        input_grad,
        cut(0, rows),
        cut(rows, rows),
        grad_wide,
        cut(5 * rows, 3 * rows),
        grad_dense,
        bias_sum,
        cut(2 * rows, rows),
        cut(3 * rows, rows),
        grad_tall,
        cut(8 * rows, units),
        grad_back,
        bias_sum,
    )


def solution(mesh):
    copies = mesh.shape["batch"] // 4
    inner = Mesh(mesh.devices.reshape(2, 2, copies, 2, 2), AXES)
    batch, ctx = AXES[:3], AXES[3:]
    tokens = P(batch, ctx, None)
    vector, matrix = P(AXES), P(AXES, None)
    params = (vector, vector, matrix, vector, matrix, vector)
    return jax.shard_map(
        functools.partial(shards, copies),
        mesh=inner,
        in_specs=(tokens, tokens, P(batch, None), P(batch, None)) + params + params,
        out_specs=(tokens, tokens) + params + params,
        check_vma=False,
    )
```
